32 devices in a mesh: parts: 2 (over y), seq: 8 (over z, x), dp: 2 (over core).
Axes of the slice: x: 2, y: 2, z: 4, core: 2. Of those that a mesh axis runs over, the one named last changes fastest.
Arguments:
- inputs: bfloat16 [4, 1024, 768], P(('parts', 'dp'), 'seq'), parts along dimension 0, may hold values from -6 to 6
- cotangent: bfloat16 [4, 1024, 768], P(('parts', 'dp'), 'seq'), parts along dimension 0, may hold values from -6 to 6
- up_weight: bfloat16 [768, 1536], P(None, 'dp'), may hold values from -0.21875 to 0.21875
- down_weight: bfloat16 [1536, 768], P('dp'), may hold values from -0.15625 to 0.15625
- first_gain: float32 [768], replicated, may hold values from 0.5 to 1.5
- first_bias: float32 [768], replicated, may hold values from -3 to 3
- up_bias: float32 [1536], replicated, may hold values from -3 to 3
- down_bias: float32 [768], replicated, may hold values from -3 to 3
- second_gain: float32 [768], replicated, may hold values from 0.5 to 1.5
Outputs:
- grad_inputs: bfloat16 [4, 1024, 768], P(('parts', 'dp'), 'seq'), parts along dimension 0
- grad_first_gain: float32 [1536], P('parts'), parts along dimension 0
- grad_first_bias: float32 [1536], P('parts'), parts along dimension 0
- grad_up_bias: float32 [3072], P('parts'), parts along dimension 0
- grad_down_bias: float32 [1536], P('parts'), parts along dimension 0
- grad_second_gain: float32 [1536], P('parts'), parts along dimension 0
The draws below stay inside these ranges and needn't reach their ends.
There are 2 independent parts, one for each index of `parts`. The reference program is written for one: setup_inputs(seed, part) draws one part's arguments, and reference() takes and returns one part's arrays. A program takes and returns all parts, laid end to end along the dimension named above; an argument that names none is the same for every part. Nothing has to cross between parts.
All inputs are finite; a program needn't handle non-finite values.
Results may differ from the reference program's by a relative error of at most 0.0095.
Values may be sent and summed in bfloat16 or wider, within the bound.
A program may use at most 64 MiB of HBM per device.

```python
import math
import jax
import jax.numpy as jnp
from jax import lax

D = 768
FF = 1536
TOK_DEV = 128
FACTOR = 8
LENGTH = 1024
DOCS = 2


def block_scale(stream_key, extent, split, least, high):
    gain, own = 1.0, jax.random.fold_in(stream_key, 6)
    for axis_at, blocks in split:
        steps = jnp.exp(jax.random.uniform(jax.random.fold_in(own, axis_at), (blocks,), jnp.float32, least / len(split), high / len(split)))
        gain = gain * jnp.repeat(steps, extent[axis_at] // blocks).reshape([-1 if axis == axis_at else 1 for axis in range(len(extent))])
    return gain


def bell_draw(key, dims, scale, reach, cuts=(), kind=jnp.bfloat16):
    factor_of = block_scale(key, dims, cuts, -0.22, 0.18) if cuts else 1.0
    values = jax.random.normal(key, dims, jnp.float32) * scale * factor_of
    return jnp.minimum(jnp.maximum(values, -reach), reach).astype(kind)


def setup_inputs(seed: int = 0, part: int = 0) -> dict:
    splits = jax.random.split(jax.random.key(seed), 10)
    part_splits = jax.random.split(jax.random.fold_in(splits[9], part), 10)
    return {
        "inputs": bell_draw(part_splits[0], (DOCS, LENGTH, D), 1.0, 6.0, ((0, 2), (1, 8))),
        "cotangent": bell_draw(part_splits[1], (DOCS, LENGTH, D), 1.0, 6.0, ((0, 2), (1, 8))),
        "up_weight": bell_draw(splits[2], (D, FF), D ** -0.5, 0.21875, ((1, 2),)),
        "down_weight": bell_draw(splits[3], (FF, D), FF ** -0.5, 0.15625, ((0, 2),)),
        "first_gain": jnp.clip(jax.random.uniform(splits[4], (D,), jnp.float32, 0.5, 1.5), 0.5, 1.5),
        "first_bias": bell_draw(splits[5], (D,), 0.5, 3.0, (), jnp.float32),
        "up_bias": bell_draw(splits[6], (FF,), 0.5, 3.0, (), jnp.float32),
        "down_bias": bell_draw(splits[7], (D,), 0.5, 3.0, (), jnp.float32),
        "second_gain": jnp.clip(jax.random.uniform(splits[8], (D,), jnp.float32, 0.5, 1.5), 0.5, 1.5),
    }


def hidden_table(width):
    index = jnp.arange(width, dtype=jnp.int32)
    angle = (index[:, None] * index[None, :] % width).astype(jnp.float32) * (2.0 * math.pi / width)
    scale = 1.0 / math.sqrt(width)
    return (jnp.concatenate([jnp.cos(angle), -jnp.sin(angle)], axis=1) * scale).astype(jnp.bfloat16)

def cross_table(shards):
    index = jnp.arange(shards, dtype=jnp.int32)
    angle = (index[:, None] * index[None, :] % shards).astype(jnp.float32) * (2.0 * math.pi / shards)
    scale = 1.0 / math.sqrt(shards)
    cosine = jnp.cos(angle) * scale
    sine = jnp.sin(angle) * scale
    upper = jnp.stack([cosine, sine], axis=2)
    lower = jnp.stack([-sine, cosine], axis=2)
    return jnp.stack([upper, lower], axis=1).astype(jnp.bfloat16)

def local_table(seq_rows):
    index = jnp.arange(seq_rows, dtype=jnp.int32)
    angle = (index[:, None] * index[None, :] % seq_rows).astype(jnp.float32) * (2.0 * math.pi / seq_rows)
    scale = 1.0 / math.sqrt(seq_rows)
    table = jnp.stack([jnp.cos(angle), jnp.sin(angle)], axis=2) * scale
    return table.reshape(seq_rows, 2 * seq_rows).astype(jnp.bfloat16)

def twiddle_angle(first_row, count, shards, total):
    offsets = first_row + jnp.arange(count, dtype=jnp.int32)
    outer = jnp.arange(shards, dtype=jnp.int32)
    product = outer[:, None] * offsets[None, :] % total
    return product.astype(jnp.float32) * (2.0 * math.pi / total)

def layer_norm(values):
    centre = lax.optimization_barrier(jnp.mean(values, axis=-1, keepdims=True))
    centred = values - centre
    spread = lax.optimization_barrier(jnp.mean(centred * centred, axis=-1, keepdims=True))
    inv_std = lax.rsqrt(spread + 1e-05)
    return (centred * inv_std, inv_std)

def norm_backward(grad, normed, inv_std):
    first = lax.optimization_barrier(jnp.mean(grad, axis=-1, keepdims=True))
    second = lax.optimization_barrier(jnp.mean(grad * normed, axis=-1, keepdims=True))
    return inv_std * (grad - first - normed * second)

def mixing(values):
    shards = FACTOR
    seq_rows = TOK_DEV
    width = values.shape[1]
    spectral = jnp.dot(values, hidden_table(width), preferred_element_type=jnp.float32).astype(jnp.bfloat16)
    spectral = spectral.reshape(shards, seq_rows, 2, width)
    mixed = jnp.einsum('aipj,pmjd->amid', cross_table(shards).astype(jnp.float32), spectral.astype(jnp.float32))
    angle = twiddle_angle(0, seq_rows, shards, seq_rows * shards)
    cosine = jnp.cos(angle)[:, :, None]
    sine = jnp.sin(angle)[:, :, None]
    real_part = mixed[:, :, 0] * cosine + mixed[:, :, 1] * sine
    imag_part = mixed[:, :, 1] * cosine - mixed[:, :, 0] * sine
    turned = jnp.stack([real_part, imag_part], axis=2).astype(jnp.bfloat16)
    table = local_table(seq_rows).reshape(seq_rows, seq_rows, 2).astype(jnp.float32)
    output = jnp.einsum('bmc,amcd->bad', table, turned.astype(jnp.float32))
    return output.astype(jnp.bfloat16).reshape(seq_rows * shards, width)

def reference(inputs, cotangent, up_weight, down_weight, first_gain, first_bias, up_bias, down_bias, second_gain):
    grad_list = []
    sum_gain1 = jnp.zeros(first_gain.shape, jnp.float32)
    sum_bias1 = jnp.zeros(first_gain.shape, jnp.float32)
    sum_up = jnp.zeros(up_bias.shape, jnp.float32)
    sum_down = jnp.zeros(first_gain.shape, jnp.float32)
    sum_gain2 = jnp.zeros(first_gain.shape, jnp.float32)
    for document in range(inputs.shape[0]):
        values = inputs[document]
        upstream = cotangent[document].astype(jnp.float32)
        summed = values.astype(jnp.float32) + mixing(values).astype(jnp.float32)
        normed1, inv1 = layer_norm(summed)
        first_out = (normed1 * first_gain + first_bias).astype(jnp.bfloat16)
        pre = jnp.dot(first_out, up_weight, preferred_element_type=jnp.float32) + up_bias
        activated, gelu_back = jax.vjp(jax.nn.gelu, pre)
        hidden = activated.astype(jnp.bfloat16)
        second_in = first_out.astype(jnp.float32) + jnp.dot(hidden, down_weight, preferred_element_type=jnp.float32) + down_bias
        normed2, inv2 = layer_norm(second_in)
        grad_v = norm_backward(upstream * second_gain, normed2, inv2)
        grad_v_low = grad_v.astype(jnp.bfloat16)
        grad_hidden = jnp.dot(grad_v_low, down_weight.T, preferred_element_type=jnp.float32)
        grad_pre = gelu_back(grad_hidden)[0]
        grad_pre_low = grad_pre.astype(jnp.bfloat16)
        grad_first = grad_v + jnp.dot(grad_pre_low, up_weight.T, preferred_element_type=jnp.float32)
        grad_summed = norm_backward(grad_first * first_gain, normed1, inv1)
        grad_low = grad_summed.astype(jnp.bfloat16)
        grad_list.append((grad_summed + mixing(grad_low).astype(jnp.float32)).astype(jnp.bfloat16))
        sum_gain1 = sum_gain1 + lax.optimization_barrier(jnp.sum(grad_first * normed1, axis=0))
        sum_bias1 = sum_bias1 + lax.optimization_barrier(jnp.sum(grad_first, axis=0))
        sum_up = sum_up + lax.optimization_barrier(jnp.sum(grad_pre, axis=0))
        sum_down = sum_down + lax.optimization_barrier(jnp.sum(grad_v, axis=0))
        sum_gain2 = sum_gain2 + lax.optimization_barrier(jnp.sum(upstream * normed2, axis=0))
    return (jnp.stack(grad_list, axis=0), sum_gain1, sum_bias1, sum_up, sum_down, sum_gain2)
```

```python
import functools
import math

import jax
import jax.numpy as jnp
import ml_dtypes
import numpy as np
from jax import lax
from jax.experimental import pallas as pl
from jax.experimental.pallas import tpu as pltpu
from jax.sharding import PartitionSpec as P


def hidden_table(width):
    index = jnp.arange(width, dtype=jnp.int32)
    angle = (index[:, None] * index[None, :] % width).astype(jnp.float32) * (2.0 * math.pi / width)
    scale = 1.0 / math.sqrt(width)
    return (jnp.concatenate([jnp.cos(angle), -jnp.sin(angle)], axis=1) * scale).astype(jnp.bfloat16)


def cross_table(shards):
    index = jnp.arange(shards, dtype=jnp.int32)
    angle = (index[:, None] * index[None, :] % shards).astype(jnp.float32) * (
        2.0 * math.pi / shards
    )
    scale = 1.0 / math.sqrt(shards)
    cosine = jnp.cos(angle) * scale
    sine = jnp.sin(angle) * scale
    upper = jnp.stack([cosine, sine], axis=2)
    lower = jnp.stack([-sine, cosine], axis=2)
    return jnp.stack([upper, lower], axis=1).astype(jnp.bfloat16)


def local_table(seq_rows):
    index = jnp.arange(seq_rows, dtype=jnp.int32)
    angle = (index[:, None] * index[None, :] % seq_rows).astype(jnp.float32) * (
        2.0 * math.pi / seq_rows
    )
    scale = 1.0 / math.sqrt(seq_rows)
    table = jnp.stack([jnp.cos(angle), jnp.sin(angle)], axis=2) * scale
    return table.reshape(seq_rows, 2 * seq_rows).astype(jnp.bfloat16)


def twiddle_angle(first_row, count, shards, total):
    offsets = first_row + jnp.arange(count, dtype=jnp.int32)
    outer = jnp.arange(shards, dtype=jnp.int32)
    product = outer[:, None] * offsets[None, :] % total
    return product.astype(jnp.float32) * (2.0 * math.pi / total)


def layer_norm(values):
    centre = jnp.mean(values, axis=-1, keepdims=True)
    centred = values - centre
    spread = jnp.mean(centred * centred, axis=-1, keepdims=True)
    inv_std = lax.rsqrt(spread + 1e-05)
    return (centred * inv_std, inv_std)


def norm_backward(grad, normed, inv_std):
    first = jnp.mean(grad, axis=-1, keepdims=True)
    second = jnp.mean(grad * normed, axis=-1, keepdims=True)
    return inv_std * (grad - first - normed * second)


def mixing(values):
    shards = lax.axis_size("seq")
    seq_rows = values.shape[0]
    width = values.shape[1]
    block = seq_rows // shards
    table = hidden_table(width)
    spectral = jnp.dot(values, table, preferred_element_type=jnp.float32).astype(jnp.bfloat16)
    spectral = lax.all_to_all(
        spectral.reshape(seq_rows, 2, width), "seq", split_axis=0, concat_axis=0, tiled=True
    )
    spectral = spectral.reshape(shards, block, 2, width)
    mixed = jnp.einsum(
        "aipj,prjd->arid", cross_table(shards), spectral, preferred_element_type=jnp.float32
    )
    angle = twiddle_angle(lax.axis_index("seq") * block, block, shards, seq_rows * shards)
    cosine = jnp.cos(angle)[:, :, None]
    sine = jnp.sin(angle)[:, :, None]
    real_part = mixed[:, :, 0] * cosine + mixed[:, :, 1] * sine
    imag_part = mixed[:, :, 1] * cosine - mixed[:, :, 0] * sine
    turned = jnp.stack([real_part, imag_part], axis=2).astype(jnp.bfloat16)
    turned = lax.all_to_all(turned, "seq", split_axis=0, concat_axis=1, tiled=True)
    output = jnp.dot(
        local_table(seq_rows),
        turned.reshape(2 * seq_rows, width),
        preferred_element_type=jnp.float32,
    )
    output = output.astype(jnp.bfloat16).reshape(seq_rows, 1, width)
    output = lax.all_to_all(output, "seq", split_axis=0, concat_axis=1, tiled=True)
    return output.reshape(seq_rows, width)


def body(
    inputs,
    cotangent,
    up_weight,
    down_weight,
    first_gain,
    first_bias,
    up_bias,
    down_bias,
    second_gain,
):
    values = inputs[0]
    upstream = cotangent[0].astype(jnp.float32)
    contract = (((1,), (1,)), ((), ()))
    summed = values.astype(jnp.float32) + mixing(values).astype(jnp.float32)
    normed1, inv1 = layer_norm(summed)
    first_out = (normed1 * first_gain + first_bias).astype(jnp.bfloat16)
    full_up, full_down = (
        lax.all_gather(up_weight, "dp", axis=1, tiled=True),
        lax.all_gather(down_weight, "dp", axis=0, tiled=True),
    )
    pre = jnp.dot(first_out, full_up, preferred_element_type=jnp.float32) + up_bias
    activated, gelu_back = jax.vjp(jax.nn.gelu, pre)
    hidden = activated.astype(jnp.bfloat16)
    second_in = (
        first_out.astype(jnp.float32)
        + jnp.dot(hidden, full_down, preferred_element_type=jnp.float32)
        + down_bias
    )
    normed2, inv2 = layer_norm(second_in)
    grad_v = norm_backward(upstream * second_gain, normed2, inv2)
    grad_v_low = grad_v.astype(jnp.bfloat16)
    grad_hidden = lax.dot_general(
        grad_v_low, full_down, contract, preferred_element_type=jnp.float32
    )
    grad_pre = gelu_back(grad_hidden)[0]
    grad_pre_low = grad_pre.astype(jnp.bfloat16)
    grad_first = grad_v + lax.dot_general(
        grad_pre_low, full_up, contract, preferred_element_type=jnp.float32
    )
    up_total = jnp.sum(grad_pre, axis=0)
    grad_summed = norm_backward(grad_first * first_gain, normed1, inv1)
    grad_low = grad_summed.astype(jnp.bfloat16)
    grad_values = (grad_summed + mixing(grad_low).astype(jnp.float32)).astype(jnp.bfloat16)
    totals = lax.psum(
        (
            jnp.sum(grad_first * normed1, axis=0),
            jnp.sum(grad_first, axis=0),
            up_total,
            jnp.sum(grad_v, axis=0),
            jnp.sum(upstream * normed2, axis=0),
        ),
        ("seq", "dp"),
    )
    return (grad_values[None], totals[0], totals[1], totals[2], totals[3], totals[4])


MESH = pl.DeviceIdType.MESH


def packed_tables(width, shards, total):
    half = width // (2 * shards)
    grid = np.arange(width)
    freq = np.arange(width // 2)
    cos_row = freq // half * (2 * half) + freq % half
    sin_row = cos_row + half
    angle = (freq[:, None] * grid[None, :] % width) * (2.0 * np.pi / width)
    forward = np.zeros((width, width))
    forward[cos_row] = np.cos(angle)
    forward[sin_row] = np.sin(angle)
    forward[half] = np.where(grid % 2 == 0, 1.0, -1.0)
    unpack = np.zeros((width, width))
    unpack[cos_row, freq] = 1.0
    unpack[sin_row[1:], freq[1:]] = -1.0
    unpack[cos_row[1:], width - freq[1:]] = 1.0
    unpack[sin_row[1:], width - freq[1:]] = 1.0
    unpack[half, width // 2] = 1.0
    index = np.arange(total)
    angle = (index[:, None] * index[None, :] % total) * (2.0 * np.pi / total)
    low = ml_dtypes.bfloat16
    return (
        forward.astype(low),
        np.cos(angle).astype(low),
        np.sin(angle).astype(low),
        unpack.astype(low),
    )


def kernel(
    shards,
    copies,
    inputs_ref,
    cot_ref,
    forward_ref,
    gain1_ref,
    bias1_ref,
    up_bias_ref,
    down_bias_ref,
    gain2_ref,
    up_hbm,
    down_hbm,
    cos_hbm,
    sin_hbm,
    unpack_hbm,
    grad_ref,
    o_gain1,
    o_bias1,
    o_up,
    o_down,
    o_gain2,
    up_full,
    down_full,
    cos_ref,
    sin_ref,
    unpack_ref,
    spec,
    gathered,
    turned,
    back,
    sums,
    normed1_ref,
    y1_ref,
    slope_ref,
    w_send,
    w_recv,
    mix_send,
    mix_recv,
    sum_send,
    sum_recv,
    local_sem,
):
    me = lax.axis_index("seq")
    core = lax.axis_index("dp")
    rows = inputs_ref.shape[1]
    width = inputs_ref.shape[2]
    part = width // shards
    total = rows * shards
    f32, low = jnp.float32, jnp.bfloat16
    group = [(k, j) for k in range(shards) for j in range(copies) if k or j]

    barrier = pltpu.get_barrier_semaphore()
    for k, j in group:
        pl.semaphore_signal(
            barrier,
            inc=1,
            device_id={"seq": lax.rem(me + k, shards), "dp": lax.rem(core + j, copies)},
            device_id_type=MESH,
        )

    local = []
    for n, (src, dst) in enumerate(
        (
            (cos_hbm, cos_ref),
            (sin_hbm, sin_ref),
            (unpack_hbm, unpack_ref),
            (up_hbm, up_full.at[core]),
            (down_hbm, down_full.at[core]),
        )
    ):
        local.append(pltpu.make_async_copy(src, dst, local_sem.at[n]))
        local[-1].start()

    def spectrum(v, slot):
        p = lax.dot_general(
            forward_ref[...], v, (((1,), (1,)), ((), ())), preferred_element_type=f32
        )
        spec[slot] = (p * (1.0 / math.sqrt(width))).astype(low)

    def rows_of(s):
        return pl.ds(pl.multiple_of(s * part, part), part)

    def cols_of(s):
        return pl.ds(pl.multiple_of(s * rows, rows), rows)

    def exchange(slot):
        first = []
        for k in range(1, shards):
            peer = lax.rem(me + k, shards)
            first.append(
                pltpu.make_async_remote_copy(
                    src_ref=spec.at[slot, rows_of(peer), :],
                    dst_ref=gathered.at[slot, :, cols_of(me)],
                    send_sem=mix_send.at[2 * slot, k],
                    recv_sem=mix_recv.at[2 * slot, k],
                    device_id={"seq": peer},
                    device_id_type=MESH,
                )
            )
            first[-1].start()
        gathered[slot, :, cols_of(me)] = spec[slot, rows_of(me), :]
        return first

    def transform(slot, first):
        for c in first:
            c.wait_recv()
        x = gathered[slot]
        row = lax.broadcasted_iota(jnp.int32, (part, total), 0)
        half = part // 2
        odd = jnp.logical_and(
            row >= half, jnp.logical_or(row > half, jnp.broadcast_to(me, row.shape) > 0)
        )
        zero = jnp.zeros_like(x)
        y = jnp.dot(jnp.where(odd, zero, x), cos_ref[...], preferred_element_type=f32)
        y = y + jnp.dot(jnp.where(odd, x, zero), sin_ref[...], preferred_element_type=f32)
        turned[slot] = (y * (1.0 / math.sqrt(total))).astype(low)
        second = []
        for k in range(1, shards):
            peer = lax.rem(me + k, shards)
            second.append(
                pltpu.make_async_remote_copy(
                    src_ref=turned.at[slot, :, cols_of(peer)],
                    dst_ref=back.at[slot, rows_of(me), :],
                    send_sem=mix_send.at[2 * slot + 1, k],
                    recv_sem=mix_recv.at[2 * slot + 1, k],
                    device_id={"seq": peer},
                    device_id_type=MESH,
                )
            )
            second[-1].start()
        back[slot, rows_of(me), :] = turned[slot, :, cols_of(me)]
        return second

    def finish(slot, first, second):
        for c in second:
            c.wait_recv()
        out = lax.dot_general(
            back[slot], unpack_ref[...], (((0,), (0,)), ((), ())), preferred_element_type=f32
        )
        for c in first + second:
            c.wait_send()
        return out

    values = inputs_ref[0]
    spectrum(values, 0)
    pl.semaphore_wait(barrier, len(group))
    first = exchange(0)
    weights = []
    for n, (src, dst) in enumerate(((up_hbm, up_full), (down_hbm, down_full))):
        weights.append(
            pltpu.make_async_remote_copy(
                src_ref=src,
                dst_ref=dst.at[core],
                send_sem=w_send.at[n],
                recv_sem=w_recv.at[n],
                device_id={"dp": lax.rem(core + 1, copies)},
                device_id_type=MESH,
            )
        )
        weights[-1].start()
    local[0].wait()
    local[1].wait()
    second = transform(0, first)
    local[2].wait()
    u = values.astype(f32) + finish(0, first, second)

    def vector(ref, start=0):
        return ref[pl.ds(start, width)].reshape(1, width)

    def norm(v):
        centred = v - jnp.mean(v, axis=-1, keepdims=True)
        inv = lax.rsqrt(jnp.mean(centred * centred, axis=-1, keepdims=True) + 1e-05)
        return centred * inv, inv

    def norm_back(grad, normed, inv):
        a = jnp.mean(grad, axis=-1, keepdims=True)
        b = jnp.mean(grad * normed, axis=-1, keepdims=True)
        return inv * (grad - a - normed * b)

    normed1, inv1 = norm(u)
    normed1_ref[...] = normed1
    y1_ref[...] = (normed1 * vector(gain1_ref) + vector(bias1_ref)).astype(low)
    acc = y1_ref[...].astype(f32) + vector(down_bias_ref)
    local[3].wait()
    local[4].wait()
    weights[0].wait()
    weights[1].wait()
    c0, c1 = math.sqrt(2.0 / math.pi), 0.044715
    hidden_half = up_full.shape[2]
    for h in range(copies):
        pre = jnp.dot(y1_ref[...], up_full[h], preferred_element_type=f32) + up_bias_ref[
            pl.ds(h * hidden_half, hidden_half)
        ].reshape(1, hidden_half)
        square = pre * pre
        t = jnp.tanh(c0 * pre * (1.0 + c1 * square))
        up1 = 0.5 * (1.0 + t)
        slope_ref[h] = up1 + 0.5 * pre * (1.0 - t * t) * (c0 * (1.0 + 3.0 * c1 * square))
        acc = acc + jnp.dot((pre * up1).astype(low), down_full[h], preferred_element_type=f32)
    normed2, inv2 = norm(acc)
    upstream = cot_ref[0].astype(f32)
    dv = norm_back(upstream * vector(gain2_ref), normed2, inv2)
    mine = me * copies + core

    def put(at, v):
        sums[mine, pl.ds(at, 1), :] = jnp.sum(v, axis=0, keepdims=True)

    put(3, dv)
    put(4, upstream * normed2)
    dv_low = dv.astype(low)
    dy1 = dv
    for h in range(copies):
        dpre = slope_ref[h] * lax.dot_general(
            dv_low, down_full[h], (((1,), (1,)), ((), ())), preferred_element_type=f32
        )
        put(5 + h, dpre)
        dy1 = dy1 + lax.dot_general(
            dpre.astype(low), up_full[h], (((1,), (1,)), ((), ())), preferred_element_type=f32
        )
    normed1 = normed1_ref[...]
    du = norm_back(dy1 * vector(gain1_ref), normed1, inv1)
    spectrum(du.astype(low), 1)
    first = exchange(1)
    put(0, dy1 * normed1)
    put(1, dy1)
    put(2, jnp.zeros((8, width), f32))
    put(7, jnp.zeros((8, width), f32))
    shares = []
    for n, (k, j) in enumerate(group):
        shares.append(
            pltpu.make_async_remote_copy(
                src_ref=sums.at[mine],
                dst_ref=sums.at[mine],
                send_sem=sum_send.at[n],
                recv_sem=sum_recv.at[n],
                device_id={"seq": lax.rem(me + k, shards), "dp": lax.rem(core + j, copies)},
                device_id_type=MESH,
            )
        )
        shares[-1].start()
    second = transform(1, first)
    for s in shares:
        s.wait()
    whole = jnp.sum(sums[...], axis=0)
    o_gain1[...] = whole[0]
    o_bias1[...] = whole[1]
    o_down[...] = whole[3]
    o_gain2[...] = whole[4]
    for h in range(copies):
        o_up[pl.ds(h * hidden_half, hidden_half)] = whole[5 + h]
    grad_ref[0] = (du + finish(1, first, second)).astype(low)


def fused_body(
    shards,
    copies,
    inputs,
    cotangent,
    up_weight,
    down_weight,
    first_gain,
    first_bias,
    up_bias,
    down_bias,
    second_gain,
):
    rows, width = inputs.shape[1:]
    total = rows * shards
    part = width // shards
    wide = up_weight.shape[1]
    tables = packed_tables(width, shards, total)
    low, f32 = jnp.bfloat16, jnp.float32
    vmem = pl.BlockSpec(memory_space=pltpu.VMEM)
    hbm = pl.BlockSpec(memory_space=pl.ANY)
    group = shards * copies
    return pl.pallas_call(
        functools.partial(kernel, shards, copies),
        out_shape=(
            jax.ShapeDtypeStruct(inputs.shape, low),
            jax.ShapeDtypeStruct((width,), f32),
            jax.ShapeDtypeStruct((width,), f32),
            jax.ShapeDtypeStruct(up_bias.shape, f32),
            jax.ShapeDtypeStruct((width,), f32),
            jax.ShapeDtypeStruct((width,), f32),
        ),
        in_specs=[vmem] * 8 + [hbm] * 5,
        out_specs=(vmem,) * 6,
        scratch_shapes=[
            pltpu.VMEM((copies, width, wide), low),
            pltpu.VMEM((copies, wide, width), low),
            pltpu.VMEM((total, total), low),
            pltpu.VMEM((total, total), low),
            pltpu.VMEM((width, width), low),
            pltpu.VMEM((2, width, rows), low),
            pltpu.VMEM((2, part, total), low),
            pltpu.VMEM((2, part, total), low),
            pltpu.VMEM((2, width, rows), low),
            pltpu.VMEM((group, 8, width), f32),
            pltpu.VMEM((rows, width), f32),
            pltpu.VMEM((rows, width), low),
            pltpu.VMEM((copies, rows, wide), f32),
            pltpu.SemaphoreType.DMA((2,)),
            pltpu.SemaphoreType.DMA((2,)),
            pltpu.SemaphoreType.DMA((4, shards)),
            pltpu.SemaphoreType.DMA((4, shards)),
            pltpu.SemaphoreType.DMA((group,)),
            pltpu.SemaphoreType.DMA((group,)),
            pltpu.SemaphoreType.DMA((5,)),
        ],
        compiler_params=pltpu.CompilerParams(
            collective_id=0, has_side_effects=True, vmem_limit_bytes=40 * 1024 * 1024
        ),
    )(
        inputs,
        cotangent,
        tables[0],
        first_gain,
        first_bias,
        up_bias,
        down_bias,
        second_gain,
        up_weight,
        down_weight,
        tables[1],
        tables[2],
        tables[3],
    )


def solution(mesh):
    shards, copies = mesh.shape["seq"], mesh.shape["dp"]
    fused = copies == 2 and shards <= 16
    return jax.shard_map(
        functools.partial(fused_body, shards, copies) if fused else body,
        mesh=mesh,
        in_specs=(
            P(("parts", "dp"), "seq", None),
            P(("parts", "dp"), "seq", None),
            P(None, "dp"),
            P("dp", None),
            P(),
            P(),
            P(),
            P(),
            P(),
        ),
        out_specs=(
            P(("parts", "dp"), "seq", None),
            P("parts"),
            P("parts"),
            P("parts"),
            P("parts"),
            P("parts"),
        ),
        check_vma=False,
    )
```

```python
import functools
import math

import jax
import jax.numpy as jnp
import ml_dtypes
import numpy as np
from jax import lax
from jax.experimental import pallas as pl
from jax.experimental.pallas import tpu as pltpu
from jax.sharding import PartitionSpec as P


def hidden_table(width):
    index = jnp.arange(width, dtype=jnp.int32)
    angle = (index[:, None] * index[None, :] % width).astype(jnp.float32) * (2.0 * math.pi / width)
    scale = 1.0 / math.sqrt(width)
    return (jnp.concatenate([jnp.cos(angle), -jnp.sin(angle)], axis=1) * scale).astype(jnp.bfloat16)


def cross_table(shards):
    index = jnp.arange(shards, dtype=jnp.int32)
    angle = (index[:, None] * index[None, :] % shards).astype(jnp.float32) * (
        2.0 * math.pi / shards
    )
    scale = 1.0 / math.sqrt(shards)
    cosine = jnp.cos(angle) * scale
    sine = jnp.sin(angle) * scale
    upper = jnp.stack([cosine, sine], axis=2)
    lower = jnp.stack([-sine, cosine], axis=2)
    return jnp.stack([upper, lower], axis=1).astype(jnp.bfloat16)


def local_table(seq_rows):
    index = jnp.arange(seq_rows, dtype=jnp.int32)
    angle = (index[:, None] * index[None, :] % seq_rows).astype(jnp.float32) * (
        2.0 * math.pi / seq_rows
    )
    scale = 1.0 / math.sqrt(seq_rows)
    table = jnp.stack([jnp.cos(angle), jnp.sin(angle)], axis=2) * scale
    return table.reshape(seq_rows, 2 * seq_rows).astype(jnp.bfloat16)


def twiddle_angle(first_row, count, shards, total):
    offsets = first_row + jnp.arange(count, dtype=jnp.int32)
    outer = jnp.arange(shards, dtype=jnp.int32)
    product = outer[:, None] * offsets[None, :] % total
    return product.astype(jnp.float32) * (2.0 * math.pi / total)


def layer_norm(values):
    centre = jnp.mean(values, axis=-1, keepdims=True)
    centred = values - centre
    spread = jnp.mean(centred * centred, axis=-1, keepdims=True)
    inv_std = lax.rsqrt(spread + 1e-05)
    return (centred * inv_std, inv_std)


def norm_backward(grad, normed, inv_std):
    first = jnp.mean(grad, axis=-1, keepdims=True)
    second = jnp.mean(grad * normed, axis=-1, keepdims=True)
    return inv_std * (grad - first - normed * second)


def mixing(values):
    shards = lax.axis_size("seq")
    seq_rows = values.shape[0]
    width = values.shape[1]
    block = seq_rows // shards
    table = hidden_table(width)
    spectral = jnp.dot(values, table, preferred_element_type=jnp.float32).astype(jnp.bfloat16)
    spectral = lax.all_to_all(
        spectral.reshape(seq_rows, 2, width), "seq", split_axis=0, concat_axis=0, tiled=True
    )
    spectral = spectral.reshape(shards, block, 2, width)
    mixed = jnp.einsum(
        "aipj,prjd->arid", cross_table(shards), spectral, preferred_element_type=jnp.float32
    )
    angle = twiddle_angle(lax.axis_index("seq") * block, block, shards, seq_rows * shards)
    cosine = jnp.cos(angle)[:, :, None]
    sine = jnp.sin(angle)[:, :, None]
    real_part = mixed[:, :, 0] * cosine + mixed[:, :, 1] * sine
    imag_part = mixed[:, :, 1] * cosine - mixed[:, :, 0] * sine
    turned = jnp.stack([real_part, imag_part], axis=2).astype(jnp.bfloat16)
    turned = lax.all_to_all(turned, "seq", split_axis=0, concat_axis=1, tiled=True)
    output = jnp.dot(
        local_table(seq_rows),
        turned.reshape(2 * seq_rows, width),
        preferred_element_type=jnp.float32,
    )
    output = output.astype(jnp.bfloat16).reshape(seq_rows, 1, width)
    output = lax.all_to_all(output, "seq", split_axis=0, concat_axis=1, tiled=True)
    return output.reshape(seq_rows, width)


def body(
    inputs,
    cotangent,
    up_weight,
    down_weight,
    first_gain,
    first_bias,
    up_bias,
    down_bias,
    second_gain,
):
    values = inputs[0]
    upstream = cotangent[0].astype(jnp.float32)
    contract = (((1,), (1,)), ((), ()))
    summed = values.astype(jnp.float32) + mixing(values).astype(jnp.float32)
    normed1, inv1 = layer_norm(summed)
    first_out = (normed1 * first_gain + first_bias).astype(jnp.bfloat16)
    full_up, full_down = (
        lax.all_gather(up_weight, "dp", axis=1, tiled=True),
        lax.all_gather(down_weight, "dp", axis=0, tiled=True),
    )
    pre = jnp.dot(first_out, full_up, preferred_element_type=jnp.float32) + up_bias
    activated, gelu_back = jax.vjp(jax.nn.gelu, pre)
    hidden = activated.astype(jnp.bfloat16)
    second_in = (
        first_out.astype(jnp.float32)
        + jnp.dot(hidden, full_down, preferred_element_type=jnp.float32)
        + down_bias
    )
    normed2, inv2 = layer_norm(second_in)
    grad_v = norm_backward(upstream * second_gain, normed2, inv2)
    grad_v_low = grad_v.astype(jnp.bfloat16)
    grad_hidden = lax.dot_general(
        grad_v_low, full_down, contract, preferred_element_type=jnp.float32
    )
    grad_pre = gelu_back(grad_hidden)[0]
    grad_pre_low = grad_pre.astype(jnp.bfloat16)
    grad_first = grad_v + lax.dot_general(
        grad_pre_low, full_up, contract, preferred_element_type=jnp.float32
    )
    up_total = jnp.sum(grad_pre, axis=0)
    grad_summed = norm_backward(grad_first * first_gain, normed1, inv1)
    grad_low = grad_summed.astype(jnp.bfloat16)
    grad_values = (grad_summed + mixing(grad_low).astype(jnp.float32)).astype(jnp.bfloat16)
    totals = lax.psum(
        (
            jnp.sum(grad_first * normed1, axis=0),
            jnp.sum(grad_first, axis=0),
            up_total,
            jnp.sum(grad_v, axis=0),
            jnp.sum(upstream * normed2, axis=0),
        ),
        ("seq", "dp"),
    )
    return (grad_values[None], totals[0], totals[1], totals[2], totals[3], totals[4])


MESH = pl.DeviceIdType.MESH


def packed_tables(width, shards, total):
    half = width // (2 * shards)
    grid = np.arange(width)
    freq = np.arange(width // 2)
    cos_row = freq // half * (2 * half) + freq % half
    sin_row = cos_row + half
    angle = (freq[:, None] * grid[None, :] % width) * (2.0 * np.pi / width)
    forward = np.zeros((width, width))
    forward[cos_row] = np.cos(angle)
    forward[sin_row] = np.sin(angle)
    forward[half] = np.where(grid % 2 == 0, 1.0, -1.0)
    unpack = np.zeros((width, width))
    unpack[cos_row, freq] = 1.0
    unpack[sin_row[1:], freq[1:]] = -1.0
    unpack[cos_row[1:], width - freq[1:]] = 1.0
    unpack[sin_row[1:], width - freq[1:]] = 1.0
    unpack[half, width // 2] = 1.0
    index = np.arange(total)
    angle = (index[:, None] * index[None, :] % total) * (2.0 * np.pi / total)
    low = ml_dtypes.bfloat16
    return (
        forward.astype(low),
        np.cos(angle).astype(low),
        np.sin(angle).astype(low),
        unpack.astype(low),
    )


def kernel(
    shards,
    copies,
    inputs_ref,
    cot_ref,
    forward_ref,
    gain1_ref,
    bias1_ref,
    up_bias_ref,
    down_bias_ref,
    gain2_ref,
    up_hbm,
    down_hbm,
    cos_hbm,
    sin_hbm,
    unpack_hbm,
    grad_ref,
    o_gain1,
    o_bias1,
    o_up,
    o_down,
    o_gain2,
    up_full,
    down_full,
    cos_ref,
    sin_ref,
    unpack_ref,
    spec,
    gathered,
    turned,
    back,
    sums,
    shared,
    summed,
    normed1_ref,
    y1_ref,
    slope_ref,
    w_send,
    w_recv,
    mix_send,
    mix_recv,
    sum_send,
    sum_recv,
    all_send,
    all_recv,
    local_sem,
):
    me = lax.axis_index("seq")
    core = lax.axis_index("dp")
    rows = inputs_ref.shape[1]
    width = inputs_ref.shape[2]
    part = width // shards
    total = rows * shards
    f32, low = jnp.float32, jnp.bfloat16
    group = [(k, j) for k in range(shards) for j in range(copies) if k or j]

    barrier = pltpu.get_barrier_semaphore()
    for k, j in group:
        pl.semaphore_signal(
            barrier,
            inc=1,
            device_id={"seq": lax.rem(me + k, shards), "dp": lax.rem(core + j, copies)},
            device_id_type=MESH,
        )

    local = []
    for n, (src, dst) in enumerate(
        (
            (cos_hbm, cos_ref),
            (sin_hbm, sin_ref),
            (unpack_hbm, unpack_ref),
            (up_hbm, up_full.at[core]),
            (down_hbm, down_full.at[core]),
        )
    ):
        local.append(pltpu.make_async_copy(src, dst, local_sem.at[n]))
        local[-1].start()

    def spectrum(v, slot):
        p = lax.dot_general(
            forward_ref[...], v, (((1,), (1,)), ((), ())), preferred_element_type=f32
        )
        spec[slot] = (p * (1.0 / math.sqrt(width))).astype(low)

    def tile_of(s):
        return pl.ds(pl.multiple_of(s * 128, 128), 128)

    def rows_of(s):
        return pl.ds(pl.multiple_of(s * part, part), part)

    def cols_of(s):
        return pl.ds(pl.multiple_of(s * rows, rows), rows)

    def exchange(slot):
        first = []
        for k in range(1, shards):
            peer = lax.rem(me + k, shards)
            first.append(
                pltpu.make_async_remote_copy(
                    src_ref=spec.at[slot, rows_of(peer), :],
                    dst_ref=gathered.at[slot, :, cols_of(me)],
                    send_sem=mix_send.at[2 * slot, k],
                    recv_sem=mix_recv.at[2 * slot, k],
                    device_id={"seq": peer},
                    device_id_type=MESH,
                )
            )
            first[-1].start()
        gathered[slot, :, cols_of(me)] = spec[slot, rows_of(me), :]
        return first

    def transform(slot, first):
        for c in first:
            c.wait_recv()
        x = gathered[slot]
        row = lax.broadcasted_iota(jnp.int32, (part, total), 0)
        half = part // 2
        odd = jnp.logical_and(
            row >= half, jnp.logical_or(row > half, jnp.broadcast_to(me, row.shape) > 0)
        )
        zero = jnp.zeros_like(x)
        y = jnp.dot(jnp.where(odd, zero, x), cos_ref[...], preferred_element_type=f32)
        y = y + jnp.dot(jnp.where(odd, x, zero), sin_ref[...], preferred_element_type=f32)
        turned[slot] = (y * (1.0 / math.sqrt(total))).astype(low)
        second = []
        for k in range(1, shards):
            peer = lax.rem(me + k, shards)
            second.append(
                pltpu.make_async_remote_copy(
                    src_ref=turned.at[slot, :, cols_of(peer)],
                    dst_ref=back.at[slot, rows_of(me), :],
                    send_sem=mix_send.at[2 * slot + 1, k],
                    recv_sem=mix_recv.at[2 * slot + 1, k],
                    device_id={"seq": peer},
                    device_id_type=MESH,
                )
            )
            second[-1].start()
        back[slot, rows_of(me), :] = turned[slot, :, cols_of(me)]
        return second

    def finish(slot, first, second):
        for c in second:
            c.wait_recv()
        out = lax.dot_general(
            back[slot], unpack_ref[...], (((0,), (0,)), ((), ())), preferred_element_type=f32
        )
        for c in first + second:
            c.wait_send()
        return out

    values = inputs_ref[0]
    spectrum(values, 0)
    pl.semaphore_wait(barrier, len(group))
    first = exchange(0)
    weights = []
    for n, (src, dst) in enumerate(((up_hbm, up_full), (down_hbm, down_full))):
        weights.append(
            pltpu.make_async_remote_copy(
                src_ref=src,
                dst_ref=dst.at[core],
                send_sem=w_send.at[n],
                recv_sem=w_recv.at[n],
                device_id={"dp": lax.rem(core + 1, copies)},
                device_id_type=MESH,
            )
        )
        weights[-1].start()
    local[0].wait()
    local[1].wait()
    second = transform(0, first)
    local[2].wait()
    u = values.astype(f32) + finish(0, first, second)

    def vector(ref, start=0):
        return ref[pl.ds(start, width)].reshape(1, width)

    def norm(v):
        centred = v - jnp.mean(v, axis=-1, keepdims=True)
        inv = lax.rsqrt(jnp.mean(centred * centred, axis=-1, keepdims=True) + 1e-05)
        return centred * inv, inv

    def norm_back(grad, normed, inv):
        a = jnp.mean(grad, axis=-1, keepdims=True)
        b = jnp.mean(grad * normed, axis=-1, keepdims=True)
        return inv * (grad - a - normed * b)

    normed1, inv1 = norm(u)
    normed1_ref[...] = normed1
    y1_ref[...] = (normed1 * vector(gain1_ref) + vector(bias1_ref)).astype(low)
    acc = y1_ref[...].astype(f32) + vector(down_bias_ref)
    local[3].wait()
    local[4].wait()
    weights[0].wait()
    weights[1].wait()
    c0, c1 = math.sqrt(2.0 / math.pi), 0.044715
    hidden_half = up_full.shape[2]
    for h in range(copies):
        pre = jnp.dot(y1_ref[...], up_full[h], preferred_element_type=f32) + up_bias_ref[
            pl.ds(h * hidden_half, hidden_half)
        ].reshape(1, hidden_half)
        square = pre * pre
        t = jnp.tanh(c0 * pre * (1.0 + c1 * square))
        up1 = 0.5 * (1.0 + t)
        slope_ref[h] = up1 + 0.5 * pre * (1.0 - t * t) * (c0 * (1.0 + 3.0 * c1 * square))
        acc = acc + jnp.dot((pre * up1).astype(low), down_full[h], preferred_element_type=f32)
    normed2, inv2 = norm(acc)
    upstream = cot_ref[0].astype(f32)
    dv = norm_back(upstream * vector(gain2_ref), normed2, inv2)
    mine = me * copies + core

    def put(at, v):
        sums[pl.ds(at, 1), pl.ds(0, width)] = jnp.sum(v, axis=0, keepdims=True)

    sums[...] = jnp.zeros(sums.shape, f32)
    put(3, dv)
    put(4, upstream * normed2)
    dv_low = dv.astype(low)
    dy1 = dv
    for h in range(copies):
        dpre = slope_ref[h] * lax.dot_general(
            dv_low, down_full[h], (((1,), (1,)), ((), ())), preferred_element_type=f32
        )
        put(5 + h, dpre)
        dy1 = dy1 + lax.dot_general(
            dpre.astype(low), up_full[h], (((1,), (1,)), ((), ())), preferred_element_type=f32
        )
    normed1 = normed1_ref[...]
    du = norm_back(dy1 * vector(gain1_ref), normed1, inv1)
    spectrum(du.astype(low), 1)
    first = exchange(1)
    put(0, dy1 * normed1)
    put(1, dy1)
    shares = []
    for n, (k, j) in enumerate(group):
        owner = lax.rem(me + k, shards)
        shares.append(
            pltpu.make_async_remote_copy(
                src_ref=sums.at[:, tile_of(owner)],
                dst_ref=shared.at[mine],
                send_sem=sum_send.at[n],
                recv_sem=sum_recv.at[n],
                device_id={"seq": owner, "dp": lax.rem(core + j, copies)},
                device_id_type=MESH,
            )
        )
        shares[-1].start()
    shared[mine] = sums[:, tile_of(me)]
    second = transform(1, first)
    for s in shares:
        s.wait()
    summed[:, tile_of(me)] = jnp.sum(shared[...], axis=0)
    shares = []
    for k in range(1, shards):
        shares.append(
            pltpu.make_async_remote_copy(
                src_ref=summed.at[:, tile_of(me)],
                dst_ref=summed.at[:, tile_of(me)],
                send_sem=all_send.at[k],
                recv_sem=all_recv.at[k],
                device_id={"seq": lax.rem(me + k, shards)},
                device_id_type=MESH,
            )
        )
        shares[-1].start()
    mixed = finish(1, first, second)
    grad_ref[0] = (du + mixed).astype(low)
    for s in shares:
        s.wait()

    def take(at):
        return summed[at, pl.ds(0, width)]

    o_gain1[...] = take(0)
    o_bias1[...] = take(1)
    o_down[...] = take(3)
    o_gain2[...] = take(4)
    for h in range(copies):
        o_up[pl.ds(h * hidden_half, hidden_half)] = take(5 + h)


def fused_body(
    shards,
    copies,
    inputs,
    cotangent,
    up_weight,
    down_weight,
    first_gain,
    first_bias,
    up_bias,
    down_bias,
    second_gain,
):
    rows, width = inputs.shape[1:]
    total = rows * shards
    part = width // shards
    wide = up_weight.shape[1]
    tables = packed_tables(width, shards, total)
    low, f32 = jnp.bfloat16, jnp.float32
    vmem = pl.BlockSpec(memory_space=pltpu.VMEM)
    hbm = pl.BlockSpec(memory_space=pl.ANY)
    group = shards * copies
    return pl.pallas_call(
        functools.partial(kernel, shards, copies),
        out_shape=(
            jax.ShapeDtypeStruct(inputs.shape, low),
            jax.ShapeDtypeStruct((width,), f32),
            jax.ShapeDtypeStruct((width,), f32),
            jax.ShapeDtypeStruct(up_bias.shape, f32),
            jax.ShapeDtypeStruct((width,), f32),
            jax.ShapeDtypeStruct((width,), f32),
        ),
        in_specs=[vmem] * 8 + [hbm] * 5,
        out_specs=(vmem,) * 6,
        scratch_shapes=[
            pltpu.VMEM((copies, width, wide), low),
            pltpu.VMEM((copies, wide, width), low),
            pltpu.VMEM((total, total), low),
            pltpu.VMEM((total, total), low),
            pltpu.VMEM((width, width), low),
            pltpu.VMEM((2, width, rows), low),
            pltpu.VMEM((2, part, total), low),
            pltpu.VMEM((2, part, total), low),
            pltpu.VMEM((2, width, rows), low),
            pltpu.VMEM((8, shards * 128), f32),
            pltpu.VMEM((group, 8, 128), f32),
            pltpu.VMEM((8, shards * 128), f32),
            pltpu.VMEM((rows, width), f32),
            pltpu.VMEM((rows, width), low),
            pltpu.VMEM((copies, rows, wide), f32),
            pltpu.SemaphoreType.DMA((2,)),
            pltpu.SemaphoreType.DMA((2,)),
            pltpu.SemaphoreType.DMA((4, shards)),
            pltpu.SemaphoreType.DMA((4, shards)),
            pltpu.SemaphoreType.DMA((group,)),
            pltpu.SemaphoreType.DMA((group,)),
            pltpu.SemaphoreType.DMA((shards,)),
            pltpu.SemaphoreType.DMA((shards,)),
            pltpu.SemaphoreType.DMA((5,)),
        ],
        compiler_params=pltpu.CompilerParams(
            collective_id=0, has_side_effects=True, vmem_limit_bytes=60 * 1024 * 1024
        ),
    )(
        inputs,
        cotangent,
        tables[0],
        first_gain,
        first_bias,
        up_bias,
        down_bias,
        second_gain,
        up_weight,
        down_weight,
        tables[1],
        tables[2],
        tables[3],
    )


def solution(mesh):
    shards, copies = mesh.shape["seq"], mesh.shape["dp"]
    fused = copies == 2 and shards == 8
    return jax.shard_map(
        functools.partial(fused_body, shards, copies) if fused else body,
        mesh=mesh,
        in_specs=(
            P(("parts", "dp"), "seq", None),
            P(("parts", "dp"), "seq", None),
            P(None, "dp"),
            P("dp", None),
            P(),
            P(),
            P(),
            P(),
            P(),
        ),
        out_specs=(
            P(("parts", "dp"), "seq", None),
            P("parts"),
            P("parts"),
            P("parts"),
            P("parts"),
            P("parts"),
        ),
        check_vma=False,
    )
```

```python
import functools
import math

import jax
import jax.numpy as jnp
import ml_dtypes
import numpy as np
from jax import lax
from jax.experimental import pallas as pl
from jax.experimental.pallas import tpu as pltpu
from jax.sharding import PartitionSpec as P


def hidden_table(width):
    index = jnp.arange(width, dtype=jnp.int32)
    angle = (index[:, None] * index[None, :] % width).astype(jnp.float32) * (2.0 * math.pi / width)
    scale = 1.0 / math.sqrt(width)
    return (jnp.concatenate([jnp.cos(angle), -jnp.sin(angle)], axis=1) * scale).astype(jnp.bfloat16)


def cross_table(shards):
    index = jnp.arange(shards, dtype=jnp.int32)
    angle = (index[:, None] * index[None, :] % shards).astype(jnp.float32) * (
        2.0 * math.pi / shards
    )
    scale = 1.0 / math.sqrt(shards)
    cosine = jnp.cos(angle) * scale
    sine = jnp.sin(angle) * scale
    upper = jnp.stack([cosine, sine], axis=2)
    lower = jnp.stack([-sine, cosine], axis=2)
    return jnp.stack([upper, lower], axis=1).astype(jnp.bfloat16)


def local_table(seq_rows):
    index = jnp.arange(seq_rows, dtype=jnp.int32)
    angle = (index[:, None] * index[None, :] % seq_rows).astype(jnp.float32) * (
        2.0 * math.pi / seq_rows
    )
    scale = 1.0 / math.sqrt(seq_rows)
    table = jnp.stack([jnp.cos(angle), jnp.sin(angle)], axis=2) * scale
    return table.reshape(seq_rows, 2 * seq_rows).astype(jnp.bfloat16)


def twiddle_angle(first_row, count, shards, total):
    offsets = first_row + jnp.arange(count, dtype=jnp.int32)
    outer = jnp.arange(shards, dtype=jnp.int32)
    product = outer[:, None] * offsets[None, :] % total
    return product.astype(jnp.float32) * (2.0 * math.pi / total)


def layer_norm(values):
    centre = jnp.mean(values, axis=-1, keepdims=True)
    centred = values - centre
    spread = jnp.mean(centred * centred, axis=-1, keepdims=True)
    inv_std = lax.rsqrt(spread + 1e-05)
    return (centred * inv_std, inv_std)


def norm_backward(grad, normed, inv_std):
    first = jnp.mean(grad, axis=-1, keepdims=True)
    second = jnp.mean(grad * normed, axis=-1, keepdims=True)
    return inv_std * (grad - first - normed * second)


def mixing(values):
    shards = lax.axis_size("seq")
    seq_rows = values.shape[0]
    width = values.shape[1]
    block = seq_rows // shards
    table = hidden_table(width)
    spectral = jnp.dot(values, table, preferred_element_type=jnp.float32).astype(jnp.bfloat16)
    spectral = lax.all_to_all(
        spectral.reshape(seq_rows, 2, width), "seq", split_axis=0, concat_axis=0, tiled=True
    )
    spectral = spectral.reshape(shards, block, 2, width)
    mixed = jnp.einsum(
        "aipj,prjd->arid", cross_table(shards), spectral, preferred_element_type=jnp.float32
    )
    angle = twiddle_angle(lax.axis_index("seq") * block, block, shards, seq_rows * shards)
    cosine = jnp.cos(angle)[:, :, None]
    sine = jnp.sin(angle)[:, :, None]
    real_part = mixed[:, :, 0] * cosine + mixed[:, :, 1] * sine
    imag_part = mixed[:, :, 1] * cosine - mixed[:, :, 0] * sine
    turned = jnp.stack([real_part, imag_part], axis=2).astype(jnp.bfloat16)
    turned = lax.all_to_all(turned, "seq", split_axis=0, concat_axis=1, tiled=True)
    output = jnp.dot(
        local_table(seq_rows),
        turned.reshape(2 * seq_rows, width),
        preferred_element_type=jnp.float32,
    )
    output = output.astype(jnp.bfloat16).reshape(seq_rows, 1, width)
    output = lax.all_to_all(output, "seq", split_axis=0, concat_axis=1, tiled=True)
    return output.reshape(seq_rows, width)


def body(
    inputs,
    cotangent,
    up_weight,
    down_weight,
    first_gain,
    first_bias,
    up_bias,
    down_bias,
    second_gain,
):
    values = inputs[0]
    upstream = cotangent[0].astype(jnp.float32)
    contract = (((1,), (1,)), ((), ()))
    summed = values.astype(jnp.float32) + mixing(values).astype(jnp.float32)
    normed1, inv1 = layer_norm(summed)
    first_out = (normed1 * first_gain + first_bias).astype(jnp.bfloat16)
    full_up, full_down = (
        lax.all_gather(up_weight, "dp", axis=1, tiled=True),
        lax.all_gather(down_weight, "dp", axis=0, tiled=True),
    )
    pre = jnp.dot(first_out, full_up, preferred_element_type=jnp.float32) + up_bias
    activated, gelu_back = jax.vjp(jax.nn.gelu, pre)
    hidden = activated.astype(jnp.bfloat16)
    second_in = (
        first_out.astype(jnp.float32)
        + jnp.dot(hidden, full_down, preferred_element_type=jnp.float32)
        + down_bias
    )
    normed2, inv2 = layer_norm(second_in)
    grad_v = norm_backward(upstream * second_gain, normed2, inv2)
    grad_v_low = grad_v.astype(jnp.bfloat16)
    grad_hidden = lax.dot_general(
        grad_v_low, full_down, contract, preferred_element_type=jnp.float32
    )
    grad_pre = gelu_back(grad_hidden)[0]
    grad_pre_low = grad_pre.astype(jnp.bfloat16)
    grad_first = grad_v + lax.dot_general(
        grad_pre_low, full_up, contract, preferred_element_type=jnp.float32
    )
    up_total = jnp.sum(grad_pre, axis=0)
    grad_summed = norm_backward(grad_first * first_gain, normed1, inv1)
    grad_low = grad_summed.astype(jnp.bfloat16)
    grad_values = (grad_summed + mixing(grad_low).astype(jnp.float32)).astype(jnp.bfloat16)
    totals = lax.psum(
        (
            jnp.sum(grad_first * normed1, axis=0),
            jnp.sum(grad_first, axis=0),
            up_total,
            jnp.sum(grad_v, axis=0),
            jnp.sum(upstream * normed2, axis=0),
        ),
        ("seq", "dp"),
    )
    return (grad_values[None], totals[0], totals[1], totals[2], totals[3], totals[4])


MESH = pl.DeviceIdType.MESH


def packed_tables(width, shards, total):
    half = width // (2 * shards)
    grid = np.arange(width)
    freq = np.arange(width // 2)
    cos_row = freq // half * (2 * half) + freq % half
    sin_row = cos_row + half
    angle = (freq[:, None] * grid[None, :] % width) * (2.0 * np.pi / width)
    forward = np.zeros((width, width))
    forward[cos_row] = np.cos(angle)
    forward[sin_row] = np.sin(angle)
    forward[half] = np.where(grid % 2 == 0, 1.0, -1.0)
    unpack = np.zeros((width, width))
    unpack[cos_row, freq] = 1.0
    unpack[sin_row[1:], freq[1:]] = -1.0
    unpack[cos_row[1:], width - freq[1:]] = 1.0
    unpack[sin_row[1:], width - freq[1:]] = 1.0
    unpack[half, width // 2] = 1.0
    index = np.arange(total)
    angle = (index[:, None] * index[None, :] % total) * (2.0 * np.pi / total)
    low = ml_dtypes.bfloat16
    return (
        forward.astype(low),
        np.cos(angle).astype(low),
        np.sin(angle).astype(low),
        unpack.astype(low),
    )


def kernel(
    shards,
    copies,
    inputs_ref,
    cot_ref,
    forward_ref,
    gain1_ref,
    bias1_ref,
    up_bias_ref,
    down_bias_ref,
    gain2_ref,
    up_hbm,
    down_hbm,
    cos_hbm,
    sin_hbm,
    unpack_hbm,
    grad_ref,
    summed_ref,
    up_full,
    down_full,
    cos_ref,
    sin_ref,
    unpack_ref,
    spec,
    gathered,
    turned,
    back,
    sums,
    shared,
    summed,
    normed1_ref,
    y1_ref,
    slope_ref,
    w_send,
    w_recv,
    mix_send,
    mix_recv,
    sum_send,
    sum_recv,
    all_send,
    all_recv,
    local_sem,
):
    me = lax.axis_index("seq")
    core = lax.axis_index("dp")
    rows = inputs_ref.shape[1]
    width = inputs_ref.shape[2]
    part = width // shards
    total = rows * shards
    f32, low = jnp.float32, jnp.bfloat16
    group = [(k, j) for k in range(shards) for j in range(copies) if k or j]

    barrier = pltpu.get_barrier_semaphore()
    for k, j in group:
        pl.semaphore_signal(
            barrier,
            inc=1,
            device_id={"seq": lax.rem(me + k, shards), "dp": lax.rem(core + j, copies)},
            device_id_type=MESH,
        )

    local = []
    for n, (src, dst) in enumerate(
        (
            (cos_hbm, cos_ref),
            (sin_hbm, sin_ref),
            (unpack_hbm, unpack_ref),
            (up_hbm, up_full.at[core]),
            (down_hbm, down_full.at[core]),
        )
    ):
        local.append(pltpu.make_async_copy(src, dst, local_sem.at[n]))
        local[-1].start()

    def spectrum(v, slot):
        p = lax.dot_general(
            forward_ref[...], v, (((1,), (1,)), ((), ())), preferred_element_type=f32
        )
        spec[slot] = (p * (1.0 / math.sqrt(width))).astype(low)

    def tile_of(s):
        return pl.ds(pl.multiple_of(s * 128, 128), 128)

    def rows_of(s):
        return pl.ds(pl.multiple_of(s * part, part), part)

    def cols_of(s):
        return pl.ds(pl.multiple_of(s * rows, rows), rows)

    def exchange(slot):
        first = []
        for k in range(1, shards):
            peer = lax.rem(me + k, shards)
            first.append(
                pltpu.make_async_remote_copy(
                    src_ref=spec.at[slot, rows_of(peer), :],
                    dst_ref=gathered.at[slot, :, cols_of(me)],
                    send_sem=mix_send.at[2 * slot, k],
                    recv_sem=mix_recv.at[2 * slot, k],
                    device_id={"seq": peer},
                    device_id_type=MESH,
                )
            )
            first[-1].start()
        gathered[slot, :, cols_of(me)] = spec[slot, rows_of(me), :]
        return first

    def transform(slot, first):
        for c in first:
            c.wait_recv()
        x = gathered[slot]
        row = lax.broadcasted_iota(jnp.int32, (part, total), 0)
        half = part // 2
        odd = jnp.logical_and(
            row >= half, jnp.logical_or(row > half, jnp.broadcast_to(me, row.shape) > 0)
        )
        zero = jnp.zeros_like(x)
        y = jnp.dot(jnp.where(odd, zero, x), cos_ref[...], preferred_element_type=f32)
        y = y + jnp.dot(jnp.where(odd, x, zero), sin_ref[...], preferred_element_type=f32)
        turned[slot] = (y * (1.0 / math.sqrt(total))).astype(low)
        second = []
        for k in range(1, shards):
            peer = lax.rem(me + k, shards)
            second.append(
                pltpu.make_async_remote_copy(
                    src_ref=turned.at[slot, :, cols_of(peer)],
                    dst_ref=back.at[slot, rows_of(me), :],
                    send_sem=mix_send.at[2 * slot + 1, k],
                    recv_sem=mix_recv.at[2 * slot + 1, k],
                    device_id={"seq": peer},
                    device_id_type=MESH,
                )
            )
            second[-1].start()
        back[slot, rows_of(me), :] = turned[slot, :, cols_of(me)]
        return second

    def finish(slot, first, second):
        for c in second:
            c.wait_recv()
        out = lax.dot_general(
            back[slot], unpack_ref[...], (((0,), (0,)), ((), ())), preferred_element_type=f32
        )
        for c in first + second:
            c.wait_send()
        return out

    values = inputs_ref[0]
    spectrum(values, 0)
    pl.semaphore_wait(barrier, len(group))
    first = exchange(0)
    weights = []
    for n, (src, dst) in enumerate(((up_hbm, up_full), (down_hbm, down_full))):
        weights.append(
            pltpu.make_async_remote_copy(
                src_ref=src,
                dst_ref=dst.at[core],
                send_sem=w_send.at[n],
                recv_sem=w_recv.at[n],
                device_id={"dp": lax.rem(core + 1, copies)},
                device_id_type=MESH,
            )
        )
        weights[-1].start()
    local[0].wait()
    local[1].wait()
    second = transform(0, first)
    local[2].wait()
    u = values.astype(f32) + finish(0, first, second)

    def vector(ref, start=0):
        return ref[pl.ds(start, width)].reshape(1, width)

    def norm(v):
        centred = v - jnp.mean(v, axis=-1, keepdims=True)
        inv = lax.rsqrt(jnp.mean(centred * centred, axis=-1, keepdims=True) + 1e-05)
        return centred * inv, inv

    def norm_back(grad, normed, inv):
        a = jnp.mean(grad, axis=-1, keepdims=True)
        b = jnp.mean(grad * normed, axis=-1, keepdims=True)
        return inv * (grad - a - normed * b)

    normed1, inv1 = norm(u)
    normed1_ref[...] = normed1
    y1_ref[...] = (normed1 * vector(gain1_ref) + vector(bias1_ref)).astype(low)
    acc = y1_ref[...].astype(f32) + vector(down_bias_ref)
    local[3].wait()
    local[4].wait()
    weights[0].wait()
    weights[1].wait()
    c0, c1 = math.sqrt(2.0 / math.pi), 0.044715
    hidden_half = up_full.shape[2]
    for h in range(copies):
        pre = jnp.dot(y1_ref[...], up_full[h], preferred_element_type=f32) + up_bias_ref[
            pl.ds(h * hidden_half, hidden_half)
        ].reshape(1, hidden_half)
        square = pre * pre
        t = jnp.tanh(c0 * pre * (1.0 + c1 * square))
        up1 = 0.5 * (1.0 + t)
        slope_ref[h] = up1 + 0.5 * pre * (1.0 - t * t) * (c0 * (1.0 + 3.0 * c1 * square))
        acc = acc + jnp.dot((pre * up1).astype(low), down_full[h], preferred_element_type=f32)
    normed2, inv2 = norm(acc)
    upstream = cot_ref[0].astype(f32)
    dv = norm_back(upstream * vector(gain2_ref), normed2, inv2)
    mine = me * copies + core

    def put(at, v):
        sums[pl.ds(at, 1), pl.ds(0, width)] = jnp.sum(v, axis=0, keepdims=True)

    sums[...] = jnp.zeros(sums.shape, f32)
    put(3, dv)
    put(4, upstream * normed2)
    dv_low = dv.astype(low)
    dy1 = dv
    for h in range(copies):
        dpre = slope_ref[h] * lax.dot_general(
            dv_low, down_full[h], (((1,), (1,)), ((), ())), preferred_element_type=f32
        )
        put(5 + h, dpre)
        dy1 = dy1 + lax.dot_general(
            dpre.astype(low), up_full[h], (((1,), (1,)), ((), ())), preferred_element_type=f32
        )
    normed1 = normed1_ref[...]
    du = norm_back(dy1 * vector(gain1_ref), normed1, inv1)
    spectrum(du.astype(low), 1)
    first = exchange(1)
    put(0, dy1 * normed1)
    put(1, dy1)
    shares = []
    for n, (k, j) in enumerate(group):
        owner = lax.rem(me + k, shards)
        shares.append(
            pltpu.make_async_remote_copy(
                src_ref=sums.at[:, tile_of(owner)],
                dst_ref=shared.at[mine],
                send_sem=sum_send.at[n],
                recv_sem=sum_recv.at[n],
                device_id={"seq": owner, "dp": lax.rem(core + j, copies)},
                device_id_type=MESH,
            )
        )
        shares[-1].start()
    shared[mine] = sums[:, tile_of(me)]
    second = transform(1, first)
    for s in shares:
        s.wait()
    summed[:, tile_of(me)] = jnp.sum(shared[...], axis=0)
    shares = []
    for k in range(1, shards):
        shares.append(
            pltpu.make_async_remote_copy(
                src_ref=summed.at[:, tile_of(me)],
                dst_ref=summed.at[:, tile_of(me)],
                send_sem=all_send.at[k],
                recv_sem=all_recv.at[k],
                device_id={"seq": lax.rem(me + k, shards)},
                device_id_type=MESH,
            )
        )
        shares[-1].start()
    mixed = finish(1, first, second)
    grad_ref[0] = (du + mixed).astype(low)
    for s in shares:
        s.wait()

    summed_ref[...] = summed[...]


def unpack_kernel(grad, summed, o_grad, o_gain1, o_bias1, o_up, o_down, o_gain2):
    width = o_gain1.shape[0]

    def take(at):
        return summed[at, pl.ds(0, width)]

    o_grad[...] = grad[...]
    o_gain1[...] = take(0)
    o_bias1[...] = take(1)
    o_down[...] = take(3)
    o_gain2[...] = take(4)
    part = o_up.shape[0] // 2
    for h in range(2):
        o_up[pl.ds(h * part, part)] = take(5 + h)


def fused_body(
    shards,
    copies,
    inputs,
    cotangent,
    up_weight,
    down_weight,
    first_gain,
    first_bias,
    up_bias,
    down_bias,
    second_gain,
):
    rows, width = inputs.shape[1:]
    total = rows * shards
    part = width // shards
    wide = up_weight.shape[1]
    tables = packed_tables(width, shards, total)
    low, f32 = jnp.bfloat16, jnp.float32
    vmem = pl.BlockSpec(memory_space=pltpu.VMEM)
    hbm = pl.BlockSpec(memory_space=pl.ANY)
    group = shards * copies
    packed = pl.pallas_call(
        functools.partial(kernel, shards, copies),
        out_shape=(
            jax.ShapeDtypeStruct(inputs.shape, low),
            jax.ShapeDtypeStruct((8, shards * 128), f32),
        ),
        in_specs=[vmem] * 8 + [hbm] * 5,
        out_specs=(vmem,) * 2,
        scratch_shapes=[
            pltpu.VMEM((copies, width, wide), low),
            pltpu.VMEM((copies, wide, width), low),
            pltpu.VMEM((total, total), low),
            pltpu.VMEM((total, total), low),
            pltpu.VMEM((width, width), low),
            pltpu.VMEM((2, width, rows), low),
            pltpu.VMEM((2, part, total), low),
            pltpu.VMEM((2, part, total), low),
            pltpu.VMEM((2, width, rows), low),
            pltpu.VMEM((8, shards * 128), f32),
            pltpu.VMEM((group, 8, 128), f32),
            pltpu.VMEM((8, shards * 128), f32),
            pltpu.VMEM((rows, width), f32),
            pltpu.VMEM((rows, width), low),
            pltpu.VMEM((copies, rows, wide), f32),
            pltpu.SemaphoreType.DMA((2,)),
            pltpu.SemaphoreType.DMA((2,)),
            pltpu.SemaphoreType.DMA((4, shards)),
            pltpu.SemaphoreType.DMA((4, shards)),
            pltpu.SemaphoreType.DMA((group,)),
            pltpu.SemaphoreType.DMA((group,)),
            pltpu.SemaphoreType.DMA((shards,)),
            pltpu.SemaphoreType.DMA((shards,)),
            pltpu.SemaphoreType.DMA((5,)),
        ],
        compiler_params=pltpu.CompilerParams(
            collective_id=0, has_side_effects=True, vmem_limit_bytes=60 * 1024 * 1024
        ),
    )(
        inputs,
        cotangent,
        tables[0],
        first_gain,
        first_bias,
        up_bias,
        down_bias,
        second_gain,
        up_weight,
        down_weight,
        tables[1],
        tables[2],
        tables[3],
    )
    return pl.pallas_call(
        unpack_kernel,
        out_shape=(
            jax.ShapeDtypeStruct(inputs.shape, low),
            jax.ShapeDtypeStruct((width,), f32),
            jax.ShapeDtypeStruct((width,), f32),
            jax.ShapeDtypeStruct(up_bias.shape, f32),
            jax.ShapeDtypeStruct((width,), f32),
            jax.ShapeDtypeStruct((width,), f32),
        ),
        in_specs=[vmem] * 2,
        out_specs=(vmem,) * 6,
        compiler_params=pltpu.CompilerParams(vmem_limit_bytes=60 * 1024 * 1024),
    )(*packed)


def solution(mesh):
    shards, copies = mesh.shape["seq"], mesh.shape["dp"]
    fused = copies == 2 and shards == 8
    return jax.shard_map(
        functools.partial(fused_body, shards, copies) if fused else body,
        mesh=mesh,
        in_specs=(
            P(("parts", "dp"), "seq", None),
            P(("parts", "dp"), "seq", None),
            P(None, "dp"),
            P("dp", None),
            P(),
            P(),
            P(),
            P(),
            P(),
        ),
        out_specs=(
            P(("parts", "dp"), "seq", None),
            P("parts"),
            P("parts"),
            P("parts"),
            P("parts"),
            P("parts"),
        ),
        check_vma=False,
    )
```

```python
import functools
import math

import jax
import jax.numpy as jnp
import ml_dtypes
import numpy as np
from jax import lax
from jax.experimental import pallas as pl
from jax.experimental.pallas import tpu as pltpu
from jax.sharding import PartitionSpec as P


def hidden_table(width):
    index = jnp.arange(width, dtype=jnp.int32)
    angle = (index[:, None] * index[None, :] % width).astype(jnp.float32) * (2.0 * math.pi / width)
    scale = 1.0 / math.sqrt(width)
    return (jnp.concatenate([jnp.cos(angle), -jnp.sin(angle)], axis=1) * scale).astype(jnp.bfloat16)


def cross_table(shards):
    index = jnp.arange(shards, dtype=jnp.int32)
    angle = (index[:, None] * index[None, :] % shards).astype(jnp.float32) * (
        2.0 * math.pi / shards
    )
    scale = 1.0 / math.sqrt(shards)
    cosine = jnp.cos(angle) * scale
    sine = jnp.sin(angle) * scale
    upper = jnp.stack([cosine, sine], axis=2)
    lower = jnp.stack([-sine, cosine], axis=2)
    return jnp.stack([upper, lower], axis=1).astype(jnp.bfloat16)


def local_table(seq_rows):
    index = jnp.arange(seq_rows, dtype=jnp.int32)
    angle = (index[:, None] * index[None, :] % seq_rows).astype(jnp.float32) * (
        2.0 * math.pi / seq_rows
    )
    scale = 1.0 / math.sqrt(seq_rows)
    table = jnp.stack([jnp.cos(angle), jnp.sin(angle)], axis=2) * scale
    return table.reshape(seq_rows, 2 * seq_rows).astype(jnp.bfloat16)


def twiddle_angle(first_row, count, shards, total):
    offsets = first_row + jnp.arange(count, dtype=jnp.int32)
    outer = jnp.arange(shards, dtype=jnp.int32)
    product = outer[:, None] * offsets[None, :] % total
    return product.astype(jnp.float32) * (2.0 * math.pi / total)


def layer_norm(values):
    centre = jnp.mean(values, axis=-1, keepdims=True)
    centred = values - centre
    spread = jnp.mean(centred * centred, axis=-1, keepdims=True)
    inv_std = lax.rsqrt(spread + 1e-05)
    return (centred * inv_std, inv_std)


def norm_backward(grad, normed, inv_std):
    first = jnp.mean(grad, axis=-1, keepdims=True)
    second = jnp.mean(grad * normed, axis=-1, keepdims=True)
    return inv_std * (grad - first - normed * second)


def mixing(values):
    shards = lax.axis_size("seq")
    seq_rows = values.shape[0]
    width = values.shape[1]
    block = seq_rows // shards
    table = hidden_table(width)
    spectral = jnp.dot(values, table, preferred_element_type=jnp.float32).astype(jnp.bfloat16)
    spectral = lax.all_to_all(
        spectral.reshape(seq_rows, 2, width), "seq", split_axis=0, concat_axis=0, tiled=True
    )
    spectral = spectral.reshape(shards, block, 2, width)
    mixed = jnp.einsum(
        "aipj,prjd->arid", cross_table(shards), spectral, preferred_element_type=jnp.float32
    )
    angle = twiddle_angle(lax.axis_index("seq") * block, block, shards, seq_rows * shards)
    cosine = jnp.cos(angle)[:, :, None]
    sine = jnp.sin(angle)[:, :, None]
    real_part = mixed[:, :, 0] * cosine + mixed[:, :, 1] * sine
    imag_part = mixed[:, :, 1] * cosine - mixed[:, :, 0] * sine
    turned = jnp.stack([real_part, imag_part], axis=2).astype(jnp.bfloat16)
    turned = lax.all_to_all(turned, "seq", split_axis=0, concat_axis=1, tiled=True)
    output = jnp.dot(
        local_table(seq_rows),
        turned.reshape(2 * seq_rows, width),
        preferred_element_type=jnp.float32,
    )
    output = output.astype(jnp.bfloat16).reshape(seq_rows, 1, width)
    output = lax.all_to_all(output, "seq", split_axis=0, concat_axis=1, tiled=True)
    return output.reshape(seq_rows, width)


def body(
    inputs,
    cotangent,
    up_weight,
    down_weight,
    first_gain,
    first_bias,
    up_bias,
    down_bias,
    second_gain,
):
    values = inputs[0]
    upstream = cotangent[0].astype(jnp.float32)
    contract = (((1,), (1,)), ((), ()))
    summed = values.astype(jnp.float32) + mixing(values).astype(jnp.float32)
    normed1, inv1 = layer_norm(summed)
    first_out = (normed1 * first_gain + first_bias).astype(jnp.bfloat16)
    full_up, full_down = (
        lax.all_gather(up_weight, "dp", axis=1, tiled=True),
        lax.all_gather(down_weight, "dp", axis=0, tiled=True),
    )
    pre = jnp.dot(first_out, full_up, preferred_element_type=jnp.float32) + up_bias
    activated, gelu_back = jax.vjp(jax.nn.gelu, pre)
    hidden = activated.astype(jnp.bfloat16)
    second_in = (
        first_out.astype(jnp.float32)
        + jnp.dot(hidden, full_down, preferred_element_type=jnp.float32)
        + down_bias
    )
    normed2, inv2 = layer_norm(second_in)
    grad_v = norm_backward(upstream * second_gain, normed2, inv2)
    grad_v_low = grad_v.astype(jnp.bfloat16)
    grad_hidden = lax.dot_general(
        grad_v_low, full_down, contract, preferred_element_type=jnp.float32
    )
    grad_pre = gelu_back(grad_hidden)[0]
    grad_pre_low = grad_pre.astype(jnp.bfloat16)
    grad_first = grad_v + lax.dot_general(
        grad_pre_low, full_up, contract, preferred_element_type=jnp.float32
    )
    up_total = jnp.sum(grad_pre, axis=0)
    grad_summed = norm_backward(grad_first * first_gain, normed1, inv1)
    grad_low = grad_summed.astype(jnp.bfloat16)
    grad_values = (grad_summed + mixing(grad_low).astype(jnp.float32)).astype(jnp.bfloat16)
    totals = lax.psum(
        (
            jnp.sum(grad_first * normed1, axis=0),
            jnp.sum(grad_first, axis=0),
            up_total,
            jnp.sum(grad_v, axis=0),
            jnp.sum(upstream * normed2, axis=0),
        ),
        ("seq", "dp"),
    )
    return (grad_values[None], totals[0], totals[1], totals[2], totals[3], totals[4])


MESH = pl.DeviceIdType.MESH


def packed_tables(width, shards, total):
    half = width // (2 * shards)
    grid = np.arange(width)
    freq = np.arange(width // 2)
    cos_row = freq // half * (2 * half) + freq % half
    sin_row = cos_row + half
    angle = (freq[:, None] * grid[None, :] % width) * (2.0 * np.pi / width)
    forward = np.zeros((width, width))
    forward[cos_row] = np.cos(angle)
    forward[sin_row] = np.sin(angle)
    forward[half] = np.where(grid % 2 == 0, 1.0, -1.0)
    unpack = np.zeros((width, width))
    unpack[cos_row, freq] = 1.0
    unpack[sin_row[1:], freq[1:]] = -1.0
    unpack[cos_row[1:], width - freq[1:]] = 1.0
    unpack[sin_row[1:], width - freq[1:]] = 1.0
    unpack[half, width // 2] = 1.0
    index = np.arange(total)
    angle = (index[:, None] * index[None, :] % total) * (2.0 * np.pi / total)
    low = ml_dtypes.bfloat16
    return (
        forward.astype(low),
        np.cos(angle).astype(low),
        np.sin(angle).astype(low),
        unpack.astype(low),
    )


def kernel(
    shards,
    copies,
    inputs_ref,
    cot_ref,
    forward_ref,
    gain1_ref,
    bias1_ref,
    up_bias_ref,
    down_bias_ref,
    gain2_ref,
    up_hbm,
    down_hbm,
    cos_hbm,
    sin_hbm,
    unpack_hbm,
    grad_ref,
    summed_ref,
    up_full,
    down_full,
    cos_ref,
    sin_ref,
    unpack_ref,
    spec,
    gathered,
    turned,
    back,
    sums,
    shared,
    summed,
    normed1_ref,
    y1_ref,
    slope_ref,
    w_send,
    w_recv,
    mix_send,
    mix_recv,
    sum_send,
    sum_recv,
    all_send,
    all_recv,
    local_sem,
):
    me = lax.axis_index("seq")
    core = lax.axis_index("dp")
    rows = inputs_ref.shape[1]
    width = inputs_ref.shape[2]
    part = width // shards
    total = rows * shards
    f32, low = jnp.float32, jnp.bfloat16
    group = [(k, j) for k in range(shards) for j in range(copies) if k or j]

    barrier = pltpu.get_barrier_semaphore()
    for k, j in group:
        pl.semaphore_signal(
            barrier,
            inc=1,
            device_id={"seq": lax.rem(me + k, shards), "dp": lax.rem(core + j, copies)},
            device_id_type=MESH,
        )

    local = []
    for n, (src, dst) in enumerate(
        (
            (cos_hbm, cos_ref),
            (sin_hbm, sin_ref),
            (unpack_hbm, unpack_ref),
            (up_hbm, up_full.at[core]),
            (down_hbm, down_full.at[core]),
        )
    ):
        local.append(pltpu.make_async_copy(src, dst, local_sem.at[n]))
        local[-1].start()

    def spectrum(v, slot):
        p = lax.dot_general(
            forward_ref[...], v, (((1,), (1,)), ((), ())), preferred_element_type=f32
        )
        spec[slot] = (p * (1.0 / math.sqrt(width))).astype(low)

    def tile_of(s):
        return pl.ds(pl.multiple_of(s * 128, 128), 128)

    def rows_of(s):
        return pl.ds(pl.multiple_of(s * part, part), part)

    def cols_of(s):
        return pl.ds(pl.multiple_of(s * rows, rows), rows)

    def exchange(slot):
        first = []
        for k in range(1, shards):
            peer = lax.rem(me + k, shards)
            first.append(
                pltpu.make_async_remote_copy(
                    src_ref=spec.at[slot, rows_of(peer), :],
                    dst_ref=gathered.at[slot, :, cols_of(me)],
                    send_sem=mix_send.at[2 * slot, k],
                    recv_sem=mix_recv.at[2 * slot, k],
                    device_id={"seq": peer},
                    device_id_type=MESH,
                )
            )
            first[-1].start()
        gathered[slot, :, cols_of(me)] = spec[slot, rows_of(me), :]
        return first

    def transform(slot, first):
        for c in first:
            c.wait_recv()
        x = gathered[slot]
        row = lax.broadcasted_iota(jnp.int32, (part, total), 0)
        half = part // 2
        odd = jnp.logical_and(
            row >= half, jnp.logical_or(row > half, jnp.broadcast_to(me, row.shape) > 0)
        )
        zero = jnp.zeros_like(x)
        y = jnp.dot(jnp.where(odd, zero, x), cos_ref[...], preferred_element_type=f32)
        y = y + jnp.dot(jnp.where(odd, x, zero), sin_ref[...], preferred_element_type=f32)
        turned[slot] = (y * (1.0 / math.sqrt(total))).astype(low)
        second = []
        for k in range(1, shards):
            peer = lax.rem(me + k, shards)
            second.append(
                pltpu.make_async_remote_copy(
                    src_ref=turned.at[slot, :, cols_of(peer)],
                    dst_ref=back.at[slot, rows_of(me), :],
                    send_sem=mix_send.at[2 * slot + 1, k],
                    recv_sem=mix_recv.at[2 * slot + 1, k],
                    device_id={"seq": peer},
                    device_id_type=MESH,
                )
            )
            second[-1].start()
        back[slot, rows_of(me), :] = turned[slot, :, cols_of(me)]
        return second

    def finish(slot, first, second):
        for c in second:
            c.wait_recv()
        out = lax.dot_general(
            back[slot], unpack_ref[...], (((0,), (0,)), ((), ())), preferred_element_type=f32
        )
        for c in first + second:
            c.wait_send()
        return out

    values = inputs_ref[0]
    spectrum(values, 0)
    pl.semaphore_wait(barrier, len(group))
    first = exchange(0)
    weights = []
    for n, (src, dst) in enumerate(((up_hbm, up_full), (down_hbm, down_full))):
        weights.append(
            pltpu.make_async_remote_copy(
                src_ref=src,
                dst_ref=dst.at[core],
                send_sem=w_send.at[n],
                recv_sem=w_recv.at[n],
                device_id={"dp": lax.rem(core + 1, copies)},
                device_id_type=MESH,
            )
        )
        weights[-1].start()
    local[0].wait()
    local[1].wait()
    second = transform(0, first)
    local[2].wait()
    u = values.astype(f32) + finish(0, first, second)

    def vector(ref, start=0):
        return ref[pl.ds(start, width)].reshape(1, width)

    def norm(v):
        centred = v - jnp.mean(v, axis=-1, keepdims=True)
        inv = lax.rsqrt(jnp.mean(centred * centred, axis=-1, keepdims=True) + 1e-05)
        return centred * inv, inv

    def norm_back(grad, normed, inv):
        a = jnp.mean(grad, axis=-1, keepdims=True)
        b = jnp.mean(grad * normed, axis=-1, keepdims=True)
        return inv * (grad - a - normed * b)

    normed1, inv1 = norm(u)
    normed1_ref[...] = normed1
    y1_ref[...] = (normed1 * vector(gain1_ref) + vector(bias1_ref)).astype(low)
    acc = y1_ref[...].astype(f32) + vector(down_bias_ref)
    local[3].wait()
    local[4].wait()
    weights[0].wait()
    weights[1].wait()
    c0, c1 = math.sqrt(2.0 / math.pi), 0.044715
    hidden_half = up_full.shape[2]
    for h in range(copies):
        pre = jnp.dot(y1_ref[...], up_full[h], preferred_element_type=f32) + up_bias_ref[
            pl.ds(h * hidden_half, hidden_half)
        ].reshape(1, hidden_half)
        square = pre * pre
        t = jnp.tanh(c0 * pre * (1.0 + c1 * square))
        up1 = 0.5 * (1.0 + t)
        slope_ref[h] = up1 + 0.5 * pre * (1.0 - t * t) * (c0 * (1.0 + 3.0 * c1 * square))
        acc = acc + jnp.dot((pre * up1).astype(low), down_full[h], preferred_element_type=f32)
    normed2, inv2 = norm(acc)
    upstream = cot_ref[0].astype(f32)
    dv = norm_back(upstream * vector(gain2_ref), normed2, inv2)
    mine = me * copies + core

    def put(at, v):
        sums[pl.ds(at, 1), pl.ds(0, width)] = jnp.sum(v, axis=0, keepdims=True)

    sums[...] = jnp.zeros(sums.shape, f32)
    put(3, dv)
    put(4, upstream * normed2)
    dv_low = dv.astype(low)
    dy1 = dv
    for h in range(copies):
        dpre = slope_ref[h] * lax.dot_general(
            dv_low, down_full[h], (((1,), (1,)), ((), ())), preferred_element_type=f32
        )
        put(5 + h, dpre)
        dy1 = dy1 + lax.dot_general(
            dpre.astype(low), up_full[h], (((1,), (1,)), ((), ())), preferred_element_type=f32
        )
    normed1 = normed1_ref[...]
    du = norm_back(dy1 * vector(gain1_ref), normed1, inv1)
    put(0, dy1 * normed1)
    put(1, dy1)
    shares = []
    for n, (k, j) in enumerate(group):
        owner = lax.rem(me + k, shards)
        shares.append(
            pltpu.make_async_remote_copy(
                src_ref=sums.at[:, tile_of(owner)],
                dst_ref=shared.at[mine],
                send_sem=sum_send.at[n],
                recv_sem=sum_recv.at[n],
                device_id={"seq": owner, "dp": lax.rem(core + j, copies)},
                device_id_type=MESH,
            )
        )
        shares[-1].start()
    shared[mine] = sums[:, tile_of(me)]
    spectrum(du.astype(low), 1)
    first = exchange(1)
    for s in shares:
        s.wait()
    summed[:, tile_of(me)] = jnp.sum(shared[...], axis=0)
    shares = []
    for k in range(1, shards):
        shares.append(
            pltpu.make_async_remote_copy(
                src_ref=summed.at[:, tile_of(me)],
                dst_ref=summed.at[:, tile_of(me)],
                send_sem=all_send.at[k],
                recv_sem=all_recv.at[k],
                device_id={"seq": lax.rem(me + k, shards)},
                device_id_type=MESH,
            )
        )
        shares[-1].start()
    second = transform(1, first)
    mixed = finish(1, first, second)
    grad_ref[0] = (du + mixed).astype(low)
    for s in shares:
        s.wait()

    summed_ref[...] = summed[...]


def unpack_kernel(grad, summed, o_grad, o_gain1, o_bias1, o_up, o_down, o_gain2):
    width = o_gain1.shape[0]

    def take(at):
        return summed[at, pl.ds(0, width)]

    o_grad[...] = grad[...]
    o_gain1[...] = take(0)
    o_bias1[...] = take(1)
    o_down[...] = take(3)
    o_gain2[...] = take(4)
    part = o_up.shape[0] // 2
    for h in range(2):
        o_up[pl.ds(h * part, part)] = take(5 + h)


def fused_body(
    shards,
    copies,
    inputs,
    cotangent,
    up_weight,
    down_weight,
    first_gain,
    first_bias,
    up_bias,
    down_bias,
    second_gain,
):
    rows, width = inputs.shape[1:]
    total = rows * shards
    part = width // shards
    wide = up_weight.shape[1]
    tables = packed_tables(width, shards, total)
    low, f32 = jnp.bfloat16, jnp.float32
    vmem = pl.BlockSpec(memory_space=pltpu.VMEM)
    hbm = pl.BlockSpec(memory_space=pl.ANY)
    group = shards * copies
    packed = pl.pallas_call(
        functools.partial(kernel, shards, copies),
        out_shape=(
            jax.ShapeDtypeStruct(inputs.shape, low),
            jax.ShapeDtypeStruct((8, shards * 128), f32),
        ),
        in_specs=[vmem] * 8 + [hbm] * 5,
        out_specs=(vmem,) * 2,
        scratch_shapes=[
            pltpu.VMEM((copies, width, wide), low),
            pltpu.VMEM((copies, wide, width), low),
            pltpu.VMEM((total, total), low),
            pltpu.VMEM((total, total), low),
            pltpu.VMEM((width, width), low),
            pltpu.VMEM((2, width, rows), low),
            pltpu.VMEM((2, part, total), low),
            pltpu.VMEM((2, part, total), low),
            pltpu.VMEM((2, width, rows), low),
            pltpu.VMEM((8, shards * 128), f32),
            pltpu.VMEM((group, 8, 128), f32),
            pltpu.VMEM((8, shards * 128), f32),
            pltpu.VMEM((rows, width), f32),
            pltpu.VMEM((rows, width), low),
            pltpu.VMEM((copies, rows, wide), f32),
            pltpu.SemaphoreType.DMA((2,)),
            pltpu.SemaphoreType.DMA((2,)),
            pltpu.SemaphoreType.DMA((4, shards)),
            pltpu.SemaphoreType.DMA((4, shards)),
            pltpu.SemaphoreType.DMA((group,)),
            pltpu.SemaphoreType.DMA((group,)),
            pltpu.SemaphoreType.DMA((shards,)),
            pltpu.SemaphoreType.DMA((shards,)),
            pltpu.SemaphoreType.DMA((5,)),
        ],
        compiler_params=pltpu.CompilerParams(
            collective_id=0, has_side_effects=True, vmem_limit_bytes=60 * 1024 * 1024
        ),
    )(
        inputs,
        cotangent,
        tables[0],
        first_gain,
        first_bias,
        up_bias,
        down_bias,
        second_gain,
        up_weight,
        down_weight,
        tables[1],
        tables[2],
        tables[3],
    )
    return pl.pallas_call(
        unpack_kernel,
        out_shape=(
            jax.ShapeDtypeStruct(inputs.shape, low),
            jax.ShapeDtypeStruct((width,), f32),
            jax.ShapeDtypeStruct((width,), f32),
            jax.ShapeDtypeStruct(up_bias.shape, f32),
            jax.ShapeDtypeStruct((width,), f32),
            jax.ShapeDtypeStruct((width,), f32),
        ),
        in_specs=[vmem] * 2,
        out_specs=(vmem,) * 6,
        compiler_params=pltpu.CompilerParams(vmem_limit_bytes=60 * 1024 * 1024),
    )(*packed)


def solution(mesh):
    shards, copies = mesh.shape["seq"], mesh.shape["dp"]
    fused = copies == 2 and shards == 8
    return jax.shard_map(
        functools.partial(fused_body, shards, copies) if fused else body,
        mesh=mesh,
        in_specs=(
            P(("parts", "dp"), "seq", None),
            P(("parts", "dp"), "seq", None),
            P(None, "dp"),
            P("dp", None),
            P(),
            P(),
            P(),
            P(),
            P(),
        ),
        out_specs=(
            P(("parts", "dp"), "seq", None),
            P("parts"),
            P("parts"),
            P("parts"),
            P("parts"),
            P("parts"),
        ),
        check_vma=False,
    )
```

```python
import functools
import math

import jax
import jax.numpy as jnp
import ml_dtypes
import numpy as np
from jax import lax
from jax.experimental import pallas as pl
from jax.experimental.pallas import tpu as pltpu
from jax.sharding import PartitionSpec as P


def hidden_table(width):
    index = jnp.arange(width, dtype=jnp.int32)
    angle = (index[:, None] * index[None, :] % width).astype(jnp.float32) * (2.0 * math.pi / width)
    scale = 1.0 / math.sqrt(width)
    return (jnp.concatenate([jnp.cos(angle), -jnp.sin(angle)], axis=1) * scale).astype(jnp.bfloat16)


def cross_table(shards):
    index = jnp.arange(shards, dtype=jnp.int32)
    angle = (index[:, None] * index[None, :] % shards).astype(jnp.float32) * (
        2.0 * math.pi / shards
    )
    scale = 1.0 / math.sqrt(shards)
    cosine = jnp.cos(angle) * scale
    sine = jnp.sin(angle) * scale
    upper = jnp.stack([cosine, sine], axis=2)
    lower = jnp.stack([-sine, cosine], axis=2)
    return jnp.stack([upper, lower], axis=1).astype(jnp.bfloat16)


def local_table(seq_rows):
    index = jnp.arange(seq_rows, dtype=jnp.int32)
    angle = (index[:, None] * index[None, :] % seq_rows).astype(jnp.float32) * (
        2.0 * math.pi / seq_rows
    )
    scale = 1.0 / math.sqrt(seq_rows)
    table = jnp.stack([jnp.cos(angle), jnp.sin(angle)], axis=2) * scale
    return table.reshape(seq_rows, 2 * seq_rows).astype(jnp.bfloat16)


def twiddle_angle(first_row, count, shards, total):
    offsets = first_row + jnp.arange(count, dtype=jnp.int32)
    outer = jnp.arange(shards, dtype=jnp.int32)
    product = outer[:, None] * offsets[None, :] % total
    return product.astype(jnp.float32) * (2.0 * math.pi / total)


def layer_norm(values):
    centre = jnp.mean(values, axis=-1, keepdims=True)
    centred = values - centre
    spread = jnp.mean(centred * centred, axis=-1, keepdims=True)
    inv_std = lax.rsqrt(spread + 1e-05)
    return (centred * inv_std, inv_std)


def norm_backward(grad, normed, inv_std):
    first = jnp.mean(grad, axis=-1, keepdims=True)
    second = jnp.mean(grad * normed, axis=-1, keepdims=True)
    return inv_std * (grad - first - normed * second)


def mixing(values):
    shards = lax.axis_size("seq")
    seq_rows = values.shape[0]
    width = values.shape[1]
    block = seq_rows // shards
    table = hidden_table(width)
    spectral = jnp.dot(values, table, preferred_element_type=jnp.float32).astype(jnp.bfloat16)
    spectral = lax.all_to_all(
        spectral.reshape(seq_rows, 2, width), "seq", split_axis=0, concat_axis=0, tiled=True
    )
    spectral = spectral.reshape(shards, block, 2, width)
    mixed = jnp.einsum(
        "aipj,prjd->arid", cross_table(shards), spectral, preferred_element_type=jnp.float32
    )
    angle = twiddle_angle(lax.axis_index("seq") * block, block, shards, seq_rows * shards)
    cosine = jnp.cos(angle)[:, :, None]
    sine = jnp.sin(angle)[:, :, None]
    real_part = mixed[:, :, 0] * cosine + mixed[:, :, 1] * sine
    imag_part = mixed[:, :, 1] * cosine - mixed[:, :, 0] * sine
    turned = jnp.stack([real_part, imag_part], axis=2).astype(jnp.bfloat16)
    turned = lax.all_to_all(turned, "seq", split_axis=0, concat_axis=1, tiled=True)
    output = jnp.dot(
        local_table(seq_rows),
        turned.reshape(2 * seq_rows, width),
        preferred_element_type=jnp.float32,
    )
    output = output.astype(jnp.bfloat16).reshape(seq_rows, 1, width)
    output = lax.all_to_all(output, "seq", split_axis=0, concat_axis=1, tiled=True)
    return output.reshape(seq_rows, width)


def body(
    inputs,
    cotangent,
    up_weight,
    down_weight,
    first_gain,
    first_bias,
    up_bias,
    down_bias,
    second_gain,
):
    values = inputs[0]
    upstream = cotangent[0].astype(jnp.float32)
    contract = (((1,), (1,)), ((), ()))
    summed = values.astype(jnp.float32) + mixing(values).astype(jnp.float32)
    normed1, inv1 = layer_norm(summed)
    first_out = (normed1 * first_gain + first_bias).astype(jnp.bfloat16)
    full_up, full_down = (
        lax.all_gather(up_weight, "dp", axis=1, tiled=True),
        lax.all_gather(down_weight, "dp", axis=0, tiled=True),
    )
    pre = jnp.dot(first_out, full_up, preferred_element_type=jnp.float32) + up_bias
    activated, gelu_back = jax.vjp(jax.nn.gelu, pre)
    hidden = activated.astype(jnp.bfloat16)
    second_in = (
        first_out.astype(jnp.float32)
        + jnp.dot(hidden, full_down, preferred_element_type=jnp.float32)
        + down_bias
    )
    normed2, inv2 = layer_norm(second_in)
    grad_v = norm_backward(upstream * second_gain, normed2, inv2)
    grad_v_low = grad_v.astype(jnp.bfloat16)
    grad_hidden = lax.dot_general(
        grad_v_low, full_down, contract, preferred_element_type=jnp.float32
    )
    grad_pre = gelu_back(grad_hidden)[0]
    grad_pre_low = grad_pre.astype(jnp.bfloat16)
    grad_first = grad_v + lax.dot_general(
        grad_pre_low, full_up, contract, preferred_element_type=jnp.float32
    )
    up_total = jnp.sum(grad_pre, axis=0)
    grad_summed = norm_backward(grad_first * first_gain, normed1, inv1)
    grad_low = grad_summed.astype(jnp.bfloat16)
    grad_values = (grad_summed + mixing(grad_low).astype(jnp.float32)).astype(jnp.bfloat16)
    totals = lax.psum(
        (
            jnp.sum(grad_first * normed1, axis=0),
            jnp.sum(grad_first, axis=0),
            up_total,
            jnp.sum(grad_v, axis=0),
            jnp.sum(upstream * normed2, axis=0),
        ),
        ("seq", "dp"),
    )
    return (grad_values[None], totals[0], totals[1], totals[2], totals[3], totals[4])


MESH = pl.DeviceIdType.MESH


def packed_tables(width, shards, total):
    half = width // (2 * shards)
    grid = np.arange(width)
    freq = np.arange(width // 2)
    cos_row = freq // half * (2 * half) + freq % half
    sin_row = cos_row + half
    angle = (freq[:, None] * grid[None, :] % width) * (2.0 * np.pi / width)
    forward = np.zeros((width, width))
    forward[cos_row] = np.cos(angle)
    forward[sin_row] = np.sin(angle)
    forward[half] = np.where(grid % 2 == 0, 1.0, -1.0)
    unpack = np.zeros((width, width))
    unpack[cos_row, freq] = 1.0
    unpack[sin_row[1:], freq[1:]] = -1.0
    unpack[cos_row[1:], width - freq[1:]] = 1.0
    unpack[sin_row[1:], width - freq[1:]] = 1.0
    unpack[half, width // 2] = 1.0
    index = np.arange(total)
    angle = (index[:, None] * index[None, :] % total) * (2.0 * np.pi / total)
    low = ml_dtypes.bfloat16
    return (
        forward.astype(low),
        np.concatenate(
            [part.reshape(shards, -1, total) for part in (np.cos(angle), np.sin(angle))], axis=1
        )
        .reshape(2 * total, total)
        .astype(low),
        unpack.astype(low),
    )


def kernel(
    shards,
    copies,
    inputs_ref,
    cot_ref,
    forward_ref,
    gain1_ref,
    bias1_ref,
    up_bias_ref,
    down_bias_ref,
    gain2_ref,
    up_hbm,
    down_hbm,
    wave_hbm,
    unpack_hbm,
    grad_ref,
    summed_ref,
    up_full,
    down_full,
    wave_ref,
    unpack_ref,
    spec,
    gathered,
    turned,
    back,
    sums,
    shared,
    summed,
    normed1_ref,
    y1_ref,
    slope_ref,
    w_send,
    w_recv,
    mix_send,
    mix_recv,
    sum_send,
    sum_recv,
    all_send,
    all_recv,
    local_sem,
):
    me = lax.axis_index("seq")
    core = lax.axis_index("dp")
    rows = inputs_ref.shape[1]
    width = inputs_ref.shape[2]
    part = width // shards
    total = rows * shards
    f32, low = jnp.float32, jnp.bfloat16
    group = [(k, j) for k in range(shards) for j in range(copies) if k or j]

    barrier = pltpu.get_barrier_semaphore()
    for k, j in group:
        pl.semaphore_signal(
            barrier,
            inc=1,
            device_id={"seq": lax.rem(me + k, shards), "dp": lax.rem(core + j, copies)},
            device_id_type=MESH,
        )

    local = []
    for n, (src, dst) in enumerate(
        (
            (wave_hbm, wave_ref),
            (unpack_hbm, unpack_ref),
            (up_hbm, up_full.at[core]),
            (down_hbm, down_full.at[core]),
        )
    ):
        local.append(pltpu.make_async_copy(src, dst, local_sem.at[n]))
        local[-1].start()

    def spectrum(v, slot):
        p = lax.dot_general(
            forward_ref[...], v, (((1,), (1,)), ((), ())), preferred_element_type=f32
        )
        spec[slot] = (p * (1.0 / math.sqrt(width))).astype(low)

    def tile_of(s):
        return pl.ds(pl.multiple_of(s * 128, 128), 128)

    def rows_of(s):
        return pl.ds(pl.multiple_of(s * part, part), part)

    def cols_of(s):
        return pl.ds(pl.multiple_of(s * rows, rows), rows)

    def exchange(slot):
        first = []
        for k in range(1, shards):
            peer = lax.rem(me + k, shards)
            first.append(
                pltpu.make_async_remote_copy(
                    src_ref=spec.at[slot, rows_of(peer), :],
                    dst_ref=gathered.at[slot, :, cols_of(me)],
                    send_sem=mix_send.at[2 * slot, k],
                    recv_sem=mix_recv.at[2 * slot, k],
                    device_id={"seq": peer},
                    device_id_type=MESH,
                )
            )
            first[-1].start()
        gathered[slot, :, cols_of(me)] = spec[slot, rows_of(me), :]
        return first

    def transform(slot, first):
        row = lax.broadcasted_iota(jnp.int32, (part, rows), 0)
        half = part // 2
        odd = jnp.logical_and(
            row >= half, jnp.logical_or(row > half, jnp.broadcast_to(me, row.shape) > 0)
        )
        y = jnp.zeros((part, total), f32)
        for k, c in [(0, None)] + list(zip(range(1, shards), first)):
            if c is not None:
                c.wait_recv()
            source = lax.rem(me + shards - k, shards)
            x = gathered[slot, :, cols_of(source)]
            zero = jnp.zeros_like(x)
            both = jnp.concatenate([jnp.where(odd, zero, x), jnp.where(odd, x, zero)], axis=1)
            y = y + jnp.dot(
                both,
                wave_ref[pl.ds(pl.multiple_of(source * 2 * rows, 2 * rows), 2 * rows), :],
                preferred_element_type=f32,
            )
        turned[slot] = (y * (1.0 / math.sqrt(total))).astype(low)
        second = []
        for k in range(1, shards):
            peer = lax.rem(me + k, shards)
            second.append(
                pltpu.make_async_remote_copy(
                    src_ref=turned.at[slot, :, cols_of(peer)],
                    dst_ref=back.at[slot, rows_of(me), :],
                    send_sem=mix_send.at[2 * slot + 1, k],
                    recv_sem=mix_recv.at[2 * slot + 1, k],
                    device_id={"seq": peer},
                    device_id_type=MESH,
                )
            )
            second[-1].start()
        back[slot, rows_of(me), :] = turned[slot, :, cols_of(me)]
        return second

    def finish(slot, first, second):
        for c in second:
            c.wait_recv()
        out = lax.dot_general(
            back[slot], unpack_ref[...], (((0,), (0,)), ((), ())), preferred_element_type=f32
        )
        for c in first + second:
            c.wait_send()
        return out

    values = inputs_ref[0]
    spectrum(values, 0)
    pl.semaphore_wait(barrier, len(group))
    first = exchange(0)
    weights = []
    for n, (src, dst) in enumerate(((up_hbm, up_full), (down_hbm, down_full))):
        weights.append(
            pltpu.make_async_remote_copy(
                src_ref=src,
                dst_ref=dst.at[core],
                send_sem=w_send.at[n],
                recv_sem=w_recv.at[n],
                device_id={"dp": lax.rem(core + 1, copies)},
                device_id_type=MESH,
            )
        )
        weights[-1].start()
    local[0].wait()
    second = transform(0, first)
    local[1].wait()
    u = values.astype(f32) + finish(0, first, second)

    def vector(ref, start=0):
        return ref[pl.ds(start, width)].reshape(1, width)

    def norm(v):
        centred = v - jnp.mean(v, axis=-1, keepdims=True)
        inv = lax.rsqrt(jnp.mean(centred * centred, axis=-1, keepdims=True) + 1e-05)
        return centred * inv, inv

    def norm_back(grad, normed, inv):
        a = jnp.mean(grad, axis=-1, keepdims=True)
        b = jnp.mean(grad * normed, axis=-1, keepdims=True)
        return inv * (grad - a - normed * b)

    normed1, inv1 = norm(u)
    normed1_ref[...] = normed1
    y1_ref[...] = (normed1 * vector(gain1_ref) + vector(bias1_ref)).astype(low)
    acc = y1_ref[...].astype(f32) + vector(down_bias_ref)
    local[2].wait()
    local[3].wait()
    weights[0].wait()
    weights[1].wait()
    c0, c1 = math.sqrt(2.0 / math.pi), 0.044715
    hidden_half = up_full.shape[2]
    for h in range(copies):
        pre = jnp.dot(y1_ref[...], up_full[h], preferred_element_type=f32) + up_bias_ref[
            pl.ds(h * hidden_half, hidden_half)
        ].reshape(1, hidden_half)
        square = pre * pre
        t = jnp.tanh(c0 * pre * (1.0 + c1 * square))
        up1 = 0.5 * (1.0 + t)
        slope_ref[h] = up1 + 0.5 * pre * (1.0 - t * t) * (c0 * (1.0 + 3.0 * c1 * square))
        acc = acc + jnp.dot((pre * up1).astype(low), down_full[h], preferred_element_type=f32)
    normed2, inv2 = norm(acc)
    upstream = cot_ref[0].astype(f32)
    dv = norm_back(upstream * vector(gain2_ref), normed2, inv2)
    mine = me * copies + core

    def put(at, v):
        sums[pl.ds(at, 1), pl.ds(0, width)] = jnp.sum(v, axis=0, keepdims=True)

    sums[...] = jnp.zeros(sums.shape, f32)
    put(3, dv)
    put(4, upstream * normed2)
    dv_low = dv.astype(low)
    dy1 = dv
    for h in range(copies):
        dpre = slope_ref[h] * lax.dot_general(
            dv_low, down_full[h], (((1,), (1,)), ((), ())), preferred_element_type=f32
        )
        put(5 + h, dpre)
        dy1 = dy1 + lax.dot_general(
            dpre.astype(low), up_full[h], (((1,), (1,)), ((), ())), preferred_element_type=f32
        )
    normed1 = normed1_ref[...]
    du = norm_back(dy1 * vector(gain1_ref), normed1, inv1)
    put(0, dy1 * normed1)
    put(1, dy1)
    shares = []
    for n, (k, j) in enumerate(group):
        owner = lax.rem(me + k, shards)
        shares.append(
            pltpu.make_async_remote_copy(
                src_ref=sums.at[:, tile_of(owner)],
                dst_ref=shared.at[mine],
                send_sem=sum_send.at[n],
                recv_sem=sum_recv.at[n],
                device_id={"seq": owner, "dp": lax.rem(core + j, copies)},
                device_id_type=MESH,
            )
        )
        shares[-1].start()
    shared[mine] = sums[:, tile_of(me)]
    spectrum(du.astype(low), 1)
    first = exchange(1)
    for s in shares:
        s.wait()
    summed[:, tile_of(me)] = jnp.sum(shared[...], axis=0)
    shares = []
    for k in range(1, shards):
        shares.append(
            pltpu.make_async_remote_copy(
                src_ref=summed.at[:, tile_of(me)],
                dst_ref=summed.at[:, tile_of(me)],
                send_sem=all_send.at[k],
                recv_sem=all_recv.at[k],
                device_id={"seq": lax.rem(me + k, shards)},
                device_id_type=MESH,
            )
        )
        shares[-1].start()
    second = transform(1, first)
    mixed = finish(1, first, second)
    grad_ref[0] = (du + mixed).astype(low)
    for s in shares:
        s.wait()

    summed_ref[...] = summed[...]


def unpack_kernel(grad, summed, o_grad, o_gain1, o_bias1, o_up, o_down, o_gain2):
    width = o_gain1.shape[0]

    def take(at):
        return summed[at, pl.ds(0, width)]

    o_grad[...] = grad[...]
    o_gain1[...] = take(0)
    o_bias1[...] = take(1)
    o_down[...] = take(3)
    o_gain2[...] = take(4)
    part = o_up.shape[0] // 2
    for h in range(2):
        o_up[pl.ds(h * part, part)] = take(5 + h)


def fused_body(
    shards,
    copies,
    inputs,
    cotangent,
    up_weight,
    down_weight,
    first_gain,
    first_bias,
    up_bias,
    down_bias,
    second_gain,
):
    rows, width = inputs.shape[1:]
    total = rows * shards
    part = width // shards
    wide = up_weight.shape[1]
    tables = packed_tables(width, shards, total)
    low, f32 = jnp.bfloat16, jnp.float32
    vmem = pl.BlockSpec(memory_space=pltpu.VMEM)
    hbm = pl.BlockSpec(memory_space=pl.ANY)
    group = shards * copies
    packed = pl.pallas_call(
        functools.partial(kernel, shards, copies),
        out_shape=(
            jax.ShapeDtypeStruct(inputs.shape, low),
            jax.ShapeDtypeStruct((8, shards * 128), f32),
        ),
        in_specs=[vmem] * 8 + [hbm] * 4,
        out_specs=(vmem,) * 2,
        scratch_shapes=[
            pltpu.VMEM((copies, width, wide), low),
            pltpu.VMEM((copies, wide, width), low),
            pltpu.VMEM((2 * total, total), low),
            pltpu.VMEM((width, width), low),
            pltpu.VMEM((2, width, rows), low),
            pltpu.VMEM((2, part, total), low),
            pltpu.VMEM((2, part, total), low),
            pltpu.VMEM((2, width, rows), low),
            pltpu.VMEM((8, shards * 128), f32),
            pltpu.VMEM((group, 8, 128), f32),
            pltpu.VMEM((8, shards * 128), f32),
            pltpu.VMEM((rows, width), f32),
            pltpu.VMEM((rows, width), low),
            pltpu.VMEM((copies, rows, wide), f32),
            pltpu.SemaphoreType.DMA((2,)),
            pltpu.SemaphoreType.DMA((2,)),
            pltpu.SemaphoreType.DMA((4, shards)),
            pltpu.SemaphoreType.DMA((4, shards)),
            pltpu.SemaphoreType.DMA((group,)),
            pltpu.SemaphoreType.DMA((group,)),
            pltpu.SemaphoreType.DMA((shards,)),
            pltpu.SemaphoreType.DMA((shards,)),
            pltpu.SemaphoreType.DMA((4,)),
        ],
        compiler_params=pltpu.CompilerParams(
            collective_id=0, has_side_effects=True, vmem_limit_bytes=60 * 1024 * 1024
        ),
    )(
        inputs,
        cotangent,
        tables[0],
        first_gain,
        first_bias,
        up_bias,
        down_bias,
        second_gain,
        up_weight,
        down_weight,
        tables[1],
        tables[2],
    )
    return pl.pallas_call(
        unpack_kernel,
        out_shape=(
            jax.ShapeDtypeStruct(inputs.shape, low),
            jax.ShapeDtypeStruct((width,), f32),
            jax.ShapeDtypeStruct((width,), f32),
            jax.ShapeDtypeStruct(up_bias.shape, f32),
            jax.ShapeDtypeStruct((width,), f32),
            jax.ShapeDtypeStruct((width,), f32),
        ),
        in_specs=[vmem] * 2,
        out_specs=(vmem,) * 6,
        compiler_params=pltpu.CompilerParams(vmem_limit_bytes=60 * 1024 * 1024),
    )(*packed)


def solution(mesh):
    shards, copies = mesh.shape["seq"], mesh.shape["dp"]
    fused = copies == 2 and shards == 8
    return jax.shard_map(
        functools.partial(fused_body, shards, copies) if fused else body,
        mesh=mesh,
        in_specs=(
            P(("parts", "dp"), "seq", None),
            P(("parts", "dp"), "seq", None),
            P(None, "dp"),
            P("dp", None),
            P(),
            P(),
            P(),
            P(),
            P(),
        ),
        out_specs=(
            P(("parts", "dp"), "seq", None),
            P("parts"),
            P("parts"),
            P("parts"),
            P("parts"),
            P("parts"),
        ),
        check_vma=False,
    )
```

```python
import functools
import math

import jax
import jax.numpy as jnp
import ml_dtypes
import numpy as np
from jax import lax
from jax.experimental import pallas as pl
from jax.experimental.pallas import tpu as pltpu
from jax.sharding import PartitionSpec as P


def hidden_table(width):
    index = jnp.arange(width, dtype=jnp.int32)
    angle = (index[:, None] * index[None, :] % width).astype(jnp.float32) * (2.0 * math.pi / width)
    scale = 1.0 / math.sqrt(width)
    return (jnp.concatenate([jnp.cos(angle), -jnp.sin(angle)], axis=1) * scale).astype(jnp.bfloat16)


def cross_table(shards):
    index = jnp.arange(shards, dtype=jnp.int32)
    angle = (index[:, None] * index[None, :] % shards).astype(jnp.float32) * (
        2.0 * math.pi / shards
    )
    scale = 1.0 / math.sqrt(shards)
    cosine = jnp.cos(angle) * scale
    sine = jnp.sin(angle) * scale
    upper = jnp.stack([cosine, sine], axis=2)
    lower = jnp.stack([-sine, cosine], axis=2)
    return jnp.stack([upper, lower], axis=1).astype(jnp.bfloat16)


def local_table(seq_rows):
    index = jnp.arange(seq_rows, dtype=jnp.int32)
    angle = (index[:, None] * index[None, :] % seq_rows).astype(jnp.float32) * (
        2.0 * math.pi / seq_rows
    )
    scale = 1.0 / math.sqrt(seq_rows)
    table = jnp.stack([jnp.cos(angle), jnp.sin(angle)], axis=2) * scale
    return table.reshape(seq_rows, 2 * seq_rows).astype(jnp.bfloat16)


def twiddle_angle(first_row, count, shards, total):
    offsets = first_row + jnp.arange(count, dtype=jnp.int32)
    outer = jnp.arange(shards, dtype=jnp.int32)
    product = outer[:, None] * offsets[None, :] % total
    return product.astype(jnp.float32) * (2.0 * math.pi / total)


def layer_norm(values):
    centre = jnp.mean(values, axis=-1, keepdims=True)
    centred = values - centre
    spread = jnp.mean(centred * centred, axis=-1, keepdims=True)
    inv_std = lax.rsqrt(spread + 1e-05)
    return (centred * inv_std, inv_std)


def norm_backward(grad, normed, inv_std):
    first = jnp.mean(grad, axis=-1, keepdims=True)
    second = jnp.mean(grad * normed, axis=-1, keepdims=True)
    return inv_std * (grad - first - normed * second)


def mixing(values):
    shards = lax.axis_size("seq")
    seq_rows = values.shape[0]
    width = values.shape[1]
    block = seq_rows // shards
    table = hidden_table(width)
    spectral = jnp.dot(values, table, preferred_element_type=jnp.float32).astype(jnp.bfloat16)
    spectral = lax.all_to_all(
        spectral.reshape(seq_rows, 2, width), "seq", split_axis=0, concat_axis=0, tiled=True
    )
    spectral = spectral.reshape(shards, block, 2, width)
    mixed = jnp.einsum(
        "aipj,prjd->arid", cross_table(shards), spectral, preferred_element_type=jnp.float32
    )
    angle = twiddle_angle(lax.axis_index("seq") * block, block, shards, seq_rows * shards)
    cosine = jnp.cos(angle)[:, :, None]
    sine = jnp.sin(angle)[:, :, None]
    real_part = mixed[:, :, 0] * cosine + mixed[:, :, 1] * sine
    imag_part = mixed[:, :, 1] * cosine - mixed[:, :, 0] * sine
    turned = jnp.stack([real_part, imag_part], axis=2).astype(jnp.bfloat16)
    turned = lax.all_to_all(turned, "seq", split_axis=0, concat_axis=1, tiled=True)
    output = jnp.dot(
        local_table(seq_rows),
        turned.reshape(2 * seq_rows, width),
        preferred_element_type=jnp.float32,
    )
    output = output.astype(jnp.bfloat16).reshape(seq_rows, 1, width)
    output = lax.all_to_all(output, "seq", split_axis=0, concat_axis=1, tiled=True)
    return output.reshape(seq_rows, width)


def body(
    inputs,
    cotangent,
    up_weight,
    down_weight,
    first_gain,
    first_bias,
    up_bias,
    down_bias,
    second_gain,
):
    values = inputs[0]
    upstream = cotangent[0].astype(jnp.float32)
    contract = (((1,), (1,)), ((), ()))
    summed = values.astype(jnp.float32) + mixing(values).astype(jnp.float32)
    normed1, inv1 = layer_norm(summed)
    first_out = (normed1 * first_gain + first_bias).astype(jnp.bfloat16)
    full_up, full_down = (
        lax.all_gather(up_weight, "dp", axis=1, tiled=True),
        lax.all_gather(down_weight, "dp", axis=0, tiled=True),
    )
    pre = jnp.dot(first_out, full_up, preferred_element_type=jnp.float32) + up_bias
    activated, gelu_back = jax.vjp(jax.nn.gelu, pre)
    hidden = activated.astype(jnp.bfloat16)
    second_in = (
        first_out.astype(jnp.float32)
        + jnp.dot(hidden, full_down, preferred_element_type=jnp.float32)
        + down_bias
    )
    normed2, inv2 = layer_norm(second_in)
    grad_v = norm_backward(upstream * second_gain, normed2, inv2)
    grad_v_low = grad_v.astype(jnp.bfloat16)
    grad_hidden = lax.dot_general(
        grad_v_low, full_down, contract, preferred_element_type=jnp.float32
    )
    grad_pre = gelu_back(grad_hidden)[0]
    grad_pre_low = grad_pre.astype(jnp.bfloat16)
    grad_first = grad_v + lax.dot_general(
        grad_pre_low, full_up, contract, preferred_element_type=jnp.float32
    )
    up_total = jnp.sum(grad_pre, axis=0)
    grad_summed = norm_backward(grad_first * first_gain, normed1, inv1)
    grad_low = grad_summed.astype(jnp.bfloat16)
    grad_values = (grad_summed + mixing(grad_low).astype(jnp.float32)).astype(jnp.bfloat16)
    totals = lax.psum(
        (
            jnp.sum(grad_first * normed1, axis=0),
            jnp.sum(grad_first, axis=0),
            up_total,
            jnp.sum(grad_v, axis=0),
            jnp.sum(upstream * normed2, axis=0),
        ),
        ("seq", "dp"),
    )
    return (grad_values[None], totals[0], totals[1], totals[2], totals[3], totals[4])


MESH = pl.DeviceIdType.MESH


def packed_tables(width, shards, total):
    half = width // (2 * shards)
    grid = np.arange(width)
    freq = np.arange(width // 2)
    cos_row = freq // half * (2 * half) + freq % half
    sin_row = cos_row + half
    angle = (freq[:, None] * grid[None, :] % width) * (2.0 * np.pi / width)
    forward = np.zeros((width, width))
    forward[cos_row] = np.cos(angle)
    forward[sin_row] = np.sin(angle)
    forward[half] = np.where(grid % 2 == 0, 1.0, -1.0)
    unpack = np.zeros((width, width))
    unpack[cos_row, freq] = 1.0
    unpack[sin_row[1:], freq[1:]] = -1.0
    unpack[cos_row[1:], width - freq[1:]] = 1.0
    unpack[sin_row[1:], width - freq[1:]] = 1.0
    unpack[half, width // 2] = 1.0
    index = np.arange(total)
    angle = (index[:, None] * index[None, :] % total) * (2.0 * np.pi / total)
    low = ml_dtypes.bfloat16
    return (
        forward.astype(low),
        np.concatenate(
            [part.reshape(shards, -1, total) for part in (np.cos(angle), np.sin(angle))], axis=1
        )
        .reshape(2 * total, total)
        .astype(low),
        unpack.astype(low),
    )


def kernel(
    shards,
    copies,
    inputs_ref,
    cot_ref,
    forward_ref,
    gain1_ref,
    bias1_ref,
    up_bias_ref,
    down_bias_ref,
    gain2_ref,
    up_hbm,
    down_hbm,
    wave_hbm,
    unpack_hbm,
    grad_ref,
    summed_ref,
    up_full,
    down_full,
    wave_ref,
    unpack_ref,
    spec,
    gathered,
    turned,
    back,
    sums,
    shared,
    summed,
    normed1_ref,
    y1_ref,
    slope_ref,
    w_send,
    w_recv,
    mix_send,
    mix_recv,
    sum_send,
    sum_recv,
    all_send,
    all_recv,
    local_sem,
):
    me = lax.axis_index("seq")
    core = lax.axis_index("dp")
    rows = inputs_ref.shape[1]
    width = inputs_ref.shape[2]
    part = width // shards
    total = rows * shards
    f32, low = jnp.float32, jnp.bfloat16
    group = [(k, j) for k in range(shards) for j in range(copies) if k or j]

    barrier = pltpu.get_barrier_semaphore()
    for k, j in group:
        pl.semaphore_signal(
            barrier,
            inc=1,
            device_id={"seq": lax.rem(me + k, shards), "dp": lax.rem(core + j, copies)},
            device_id_type=MESH,
        )

    local = []
    for n, (src, dst) in enumerate(
        (
            (wave_hbm, wave_ref),
            (unpack_hbm, unpack_ref),
            (up_hbm, up_full.at[core]),
            (down_hbm, down_full.at[core]),
        )
    ):
        local.append(pltpu.make_async_copy(src, dst, local_sem.at[n]))
        local[-1].start()

    order = sorted(range(1, shards), key=lambda k: -abs(2 * k - shards))

    def spectrum(v, slot):
        p = lax.dot_general(
            forward_ref[...], v, (((1,), (1,)), ((), ())), preferred_element_type=f32
        )
        spec[slot] = (p * (1.0 / math.sqrt(width))).astype(low)

    def tile_of(s):
        return pl.ds(pl.multiple_of(s * 128, 128), 128)

    def rows_of(s):
        return pl.ds(pl.multiple_of(s * part, part), part)

    def cols_of(s):
        return pl.ds(pl.multiple_of(s * rows, rows), rows)

    def exchange(slot):
        first = []
        for k in order:
            peer = lax.rem(me + k, shards)
            first.append(
                pltpu.make_async_remote_copy(
                    src_ref=spec.at[slot, rows_of(peer), :],
                    dst_ref=gathered.at[slot, :, cols_of(me)],
                    send_sem=mix_send.at[2 * slot, k],
                    recv_sem=mix_recv.at[2 * slot, k],
                    device_id={"seq": peer},
                    device_id_type=MESH,
                )
            )
            first[-1].start()
        gathered[slot, :, cols_of(me)] = spec[slot, rows_of(me), :]
        return first

    def transform(slot, first):
        row = lax.broadcasted_iota(jnp.int32, (part, rows), 0)
        half = part // 2
        odd = jnp.logical_and(
            row >= half, jnp.logical_or(row > half, jnp.broadcast_to(me, row.shape) > 0)
        )
        y = jnp.zeros((part, total), f32)
        for k, c in [(0, None)] + list(zip(order, first)):
            if c is not None:
                c.wait_recv()
            source = lax.rem(me + shards - k, shards)
            x = gathered[slot, :, cols_of(source)]
            zero = jnp.zeros_like(x)
            both = jnp.concatenate([jnp.where(odd, zero, x), jnp.where(odd, x, zero)], axis=1)
            y = y + jnp.dot(
                both,
                wave_ref[pl.ds(pl.multiple_of(source * 2 * rows, 2 * rows), 2 * rows), :],
                preferred_element_type=f32,
            )
        turned[slot] = (y * (1.0 / math.sqrt(total))).astype(low)
        second = []
        for k in order:
            peer = lax.rem(me + k, shards)
            second.append(
                pltpu.make_async_remote_copy(
                    src_ref=turned.at[slot, :, cols_of(peer)],
                    dst_ref=back.at[slot, rows_of(me), :],
                    send_sem=mix_send.at[2 * slot + 1, k],
                    recv_sem=mix_recv.at[2 * slot + 1, k],
                    device_id={"seq": peer},
                    device_id_type=MESH,
                )
            )
            second[-1].start()
        back[slot, rows_of(me), :] = turned[slot, :, cols_of(me)]
        return second

    def finish(slot, first, second):
        for c in second:
            c.wait_recv()
        out = lax.dot_general(
            back[slot], unpack_ref[...], (((0,), (0,)), ((), ())), preferred_element_type=f32
        )
        for c in first + second:
            c.wait_send()
        return out

    values = inputs_ref[0]
    spectrum(values, 0)
    pl.semaphore_wait(barrier, len(group))
    first = exchange(0)
    weights = []
    for n, (src, dst) in enumerate(((up_hbm, up_full), (down_hbm, down_full))):
        weights.append(
            pltpu.make_async_remote_copy(
                src_ref=src,
                dst_ref=dst.at[core],
                send_sem=w_send.at[n],
                recv_sem=w_recv.at[n],
                device_id={"dp": lax.rem(core + 1, copies)},
                device_id_type=MESH,
            )
        )
        weights[-1].start()
    local[0].wait()
    second = transform(0, first)
    local[1].wait()
    u = values.astype(f32) + finish(0, first, second)

    def vector(ref, start=0):
        return ref[pl.ds(start, width)].reshape(1, width)

    def norm(v):
        centred = v - jnp.mean(v, axis=-1, keepdims=True)
        inv = lax.rsqrt(jnp.mean(centred * centred, axis=-1, keepdims=True) + 1e-05)
        return centred * inv, inv

    def norm_back(grad, normed, inv):
        a = jnp.mean(grad, axis=-1, keepdims=True)
        b = jnp.mean(grad * normed, axis=-1, keepdims=True)
        return inv * (grad - a - normed * b)

    normed1, inv1 = norm(u)
    normed1_ref[...] = normed1
    y1_ref[...] = (normed1 * vector(gain1_ref) + vector(bias1_ref)).astype(low)
    acc = y1_ref[...].astype(f32) + vector(down_bias_ref)
    local[2].wait()
    local[3].wait()
    weights[0].wait()
    weights[1].wait()
    c0, c1 = math.sqrt(2.0 / math.pi), 0.044715
    hidden_half = up_full.shape[2]
    for h in range(copies):
        pre = jnp.dot(y1_ref[...], up_full[h], preferred_element_type=f32) + up_bias_ref[
            pl.ds(h * hidden_half, hidden_half)
        ].reshape(1, hidden_half)
        square = pre * pre
        t = jnp.tanh(c0 * pre * (1.0 + c1 * square))
        up1 = 0.5 * (1.0 + t)
        slope_ref[h] = up1 + 0.5 * pre * (1.0 - t * t) * (c0 * (1.0 + 3.0 * c1 * square))
        acc = acc + jnp.dot((pre * up1).astype(low), down_full[h], preferred_element_type=f32)
    normed2, inv2 = norm(acc)
    upstream = cot_ref[0].astype(f32)
    dv = norm_back(upstream * vector(gain2_ref), normed2, inv2)
    mine = me * copies + core

    def put(at, v):
        sums[pl.ds(at, 1), pl.ds(0, width)] = jnp.sum(v, axis=0, keepdims=True)

    sums[...] = jnp.zeros(sums.shape, f32)
    put(3, dv)
    put(4, upstream * normed2)
    dv_low = dv.astype(low)
    dy1 = dv
    for h in range(copies):
        dpre = slope_ref[h] * lax.dot_general(
            dv_low, down_full[h], (((1,), (1,)), ((), ())), preferred_element_type=f32
        )
        put(5 + h, dpre)
        dy1 = dy1 + lax.dot_general(
            dpre.astype(low), up_full[h], (((1,), (1,)), ((), ())), preferred_element_type=f32
        )
    normed1 = normed1_ref[...]
    du = norm_back(dy1 * vector(gain1_ref), normed1, inv1)
    put(0, dy1 * normed1)
    put(1, dy1)
    shares = []
    for n, (k, j) in enumerate(group):
        owner = lax.rem(me + k, shards)
        shares.append(
            pltpu.make_async_remote_copy(
                src_ref=sums.at[:, tile_of(owner)],
                dst_ref=shared.at[mine],
                send_sem=sum_send.at[n],
                recv_sem=sum_recv.at[n],
                device_id={"seq": owner, "dp": lax.rem(core + j, copies)},
                device_id_type=MESH,
            )
        )
        shares[-1].start()
    shared[mine] = sums[:, tile_of(me)]
    spectrum(du.astype(low), 1)
    first = exchange(1)
    for s in shares:
        s.wait()
    summed[:, tile_of(me)] = jnp.sum(shared[...], axis=0)
    shares = []
    for k in range(1, shards):
        shares.append(
            pltpu.make_async_remote_copy(
                src_ref=summed.at[:, tile_of(me)],
                dst_ref=summed.at[:, tile_of(me)],
                send_sem=all_send.at[k],
                recv_sem=all_recv.at[k],
                device_id={"seq": lax.rem(me + k, shards)},
                device_id_type=MESH,
            )
        )
        shares[-1].start()
    second = transform(1, first)
    mixed = finish(1, first, second)
    grad_ref[0] = (du + mixed).astype(low)
    for s in shares:
        s.wait()

    summed_ref[...] = summed[...]


def unpack_kernel(grad, summed, o_grad, o_gain1, o_bias1, o_up, o_down, o_gain2):
    width = o_gain1.shape[0]

    def take(at):
        return summed[at, pl.ds(0, width)]

    o_grad[...] = grad[...]
    o_gain1[...] = take(0)
    o_bias1[...] = take(1)
    o_down[...] = take(3)
    o_gain2[...] = take(4)
    part = o_up.shape[0] // 2
    for h in range(2):
        o_up[pl.ds(h * part, part)] = take(5 + h)


def fused_body(
    shards,
    copies,
    inputs,
    cotangent,
    up_weight,
    down_weight,
    first_gain,
    first_bias,
    up_bias,
    down_bias,
    second_gain,
):
    rows, width = inputs.shape[1:]
    total = rows * shards
    part = width // shards
    wide = up_weight.shape[1]
    tables = packed_tables(width, shards, total)
    low, f32 = jnp.bfloat16, jnp.float32
    vmem = pl.BlockSpec(memory_space=pltpu.VMEM)
    hbm = pl.BlockSpec(memory_space=pl.ANY)
    group = shards * copies
    packed = pl.pallas_call(
        functools.partial(kernel, shards, copies),
        out_shape=(
            jax.ShapeDtypeStruct(inputs.shape, low),
            jax.ShapeDtypeStruct((8, shards * 128), f32),
        ),
        in_specs=[vmem] * 8 + [hbm] * 4,
        out_specs=(vmem,) * 2,
        scratch_shapes=[
            pltpu.VMEM((copies, width, wide), low),
            pltpu.VMEM((copies, wide, width), low),
            pltpu.VMEM((2 * total, total), low),
            pltpu.VMEM((width, width), low),
            pltpu.VMEM((2, width, rows), low),
            pltpu.VMEM((2, part, total), low),
            pltpu.VMEM((2, part, total), low),
            pltpu.VMEM((2, width, rows), low),
            pltpu.VMEM((8, shards * 128), f32),
            pltpu.VMEM((group, 8, 128), f32),
            pltpu.VMEM((8, shards * 128), f32),
            pltpu.VMEM((rows, width), f32),
            pltpu.VMEM((rows, width), low),
            pltpu.VMEM((copies, rows, wide), f32),
            pltpu.SemaphoreType.DMA((2,)),
            pltpu.SemaphoreType.DMA((2,)),
            pltpu.SemaphoreType.DMA((4, shards)),
            pltpu.SemaphoreType.DMA((4, shards)),
            pltpu.SemaphoreType.DMA((group,)),
            pltpu.SemaphoreType.DMA((group,)),
            pltpu.SemaphoreType.DMA((shards,)),
            pltpu.SemaphoreType.DMA((shards,)),
            pltpu.SemaphoreType.DMA((4,)),
        ],
        compiler_params=pltpu.CompilerParams(
            collective_id=0, has_side_effects=True, vmem_limit_bytes=60 * 1024 * 1024
        ),
    )(
        inputs,
        cotangent,
        tables[0],
        first_gain,
        first_bias,
        up_bias,
        down_bias,
        second_gain,
        up_weight,
        down_weight,
        tables[1],
        tables[2],
    )
    return pl.pallas_call(
        unpack_kernel,
        out_shape=(
            jax.ShapeDtypeStruct(inputs.shape, low),
            jax.ShapeDtypeStruct((width,), f32),
            jax.ShapeDtypeStruct((width,), f32),
            jax.ShapeDtypeStruct(up_bias.shape, f32),
            jax.ShapeDtypeStruct((width,), f32),
            jax.ShapeDtypeStruct((width,), f32),
        ),
        in_specs=[vmem] * 2,
        out_specs=(vmem,) * 6,
        compiler_params=pltpu.CompilerParams(vmem_limit_bytes=60 * 1024 * 1024),
    )(*packed)


def solution(mesh):
    shards, copies = mesh.shape["seq"], mesh.shape["dp"]
    fused = copies == 2 and shards == 8
    return jax.shard_map(
        functools.partial(fused_body, shards, copies) if fused else body,
        mesh=mesh,
        in_specs=(
            P(("parts", "dp"), "seq", None),
            P(("parts", "dp"), "seq", None),
            P(None, "dp"),
            P("dp", None),
            P(),
            P(),
            P(),
            P(),
            P(),
        ),
        out_specs=(
            P(("parts", "dp"), "seq", None),
            P("parts"),
            P("parts"),
            P("parts"),
            P("parts"),
            P("parts"),
        ),
        check_vma=False,
    )
```
